256 devices in a mesh: layer: 4 (over x), row: 8 (over y, core), col: 8 (over z).
Axes of the slice: x: 4, y: 4, z: 8, core: 2. Of those that a mesh axis runs over, the one named last changes fastest.
Arguments:
- blocks: bfloat16 [13, 512, 128, 128], P(None, ('row', 'col'), 'layer'), may hold values from -0.29882812 to 0.29882812
- presence: int32 [13, 512], P(None, ('row', 'col')), may hold values from 0 to 1, as said below
Outputs:
- purified: bfloat16 [13, 512, 128, 128], P(None, ('row', 'col'), 'layer')
The draws below stay inside these ranges and needn't reach their ends.
Inputs may be any that keep to these rules, and one draw needn't show every extreme that they name: `presence`: the tile on offset 0 is present in every block row.
All inputs are finite; a program needn't handle non-finite values.
Results may differ from the reference program's by a relative error of at most 0.01.
Values may be sent and summed in bfloat16 or wider, within the bound.
No kernel may reach another device: no remote copies, remote signals or barrier semaphores. Data moves between devices by JAX's collectives and lax.ppermute only.
A program may use at most 128 MiB of HBM per device.

```python
import jax
import jax.numpy as jnp

BS = 128
NBG = 512
BAND = 3
FAR = 160
DIAGS = 13


def draw_presence(key, part):
    key_band, key_level, key_far = jax.random.split(key, 3)
    band_rows = (jax.random.randint(key_band, (2 * BAND + 1, NBG), 0, 8) < 7).astype(jnp.int32)
    band_rows = band_rows.at[BAND].set(1)
    levels = jax.random.randint(key_level, (NBG // 8,), 1, 8)
    levels = jnp.repeat(levels, 8)
    far_rows = (jax.random.randint(key_far, (6, NBG), 0, 8) < levels[None, :]).astype(jnp.int32)
    return jnp.concatenate([band_rows, far_rows], axis=0).astype(jnp.int32)


def block_levels(key, shape, cuts, smallest, high):
    def one(position, shards_of):
        heights = jax.random.uniform(jax.random.fold_in(jax.random.fold_in(key, 6), position), (shards_of,), jnp.float32, smallest / len(cuts), high / len(cuts))
        return jnp.repeat(jnp.exp(heights), shape[position] // shards_of).reshape((-1,) + (1,) * (len(shape) - position - 1))

    factor_of = one(*cuts[0])
    for cut in cuts[1:]:
        factor_of = factor_of * one(*cut)
    return factor_of


def normal_values(key, shape, width, limit, cuts=(), held_as=jnp.bfloat16):
    result = width * jax.random.normal(key, shape, jnp.float32)
    if cuts:
        result = result * block_levels(key, shape, cuts, -0.22, 0.18)
    return jnp.clip(result, -limit, limit).astype(held_as)


def setup_inputs(seed: int = 0) -> dict:
    keys = jax.random.split(jax.random.key(seed), 3)
    blocks = normal_values(keys[0], (DIAGS, NBG, BS, BS), 0.05, 0.29882812, ((1, 64), (2, 4)))
    presence = draw_presence(jax.random.fold_in(keys[2], 71), 0)
    return {"blocks": blocks, "presence": presence}


def offset_table():
    values = list(range(-BAND, BAND + 1))
    values = values + [FAR - 1, FAR, FAR + 1, -FAR - 1, -FAR, -FAR + 1]
    return [value % NBG for value in values]


def pair_table(offsets):
    by_target = []
    for target_index in range(len(offsets)):
        entries = []
        for left_index in range(len(offsets)):
            for right_index in range(len(offsets)):
                if (offsets[left_index] + offsets[right_index]) % NBG == offsets[target_index]:
                    entries.append((left_index, right_index))
        by_target.append(entries)
    return by_target


def reference(blocks, presence):
    offsets = offset_table()
    by_target = pair_table(offsets)
    weight_mask = presence.astype(jnp.float32)[:, :, None, None]
    masked = blocks * presence.astype(jnp.bfloat16)[:, :, None, None]

    def product(left_tiles):
        totals = []
        for target_index in range(len(offsets)):
            total = jnp.zeros((NBG, BS, BS), jnp.float32)
            for left_index, right_index in by_target[target_index]:
                moved = jnp.roll(masked[right_index], -offsets[left_index], axis=0)
                total = total + jnp.einsum("ixz,izy->ixy", left_tiles[left_index].astype(jnp.float32), moved.astype(jnp.float32))
            totals.append(total)
        return jnp.stack(totals) * weight_mask

    second = product(masked).astype(jnp.bfloat16)
    third = product(second)
    return (3.0 * second.astype(jnp.float32) - 2.0 * third).astype(jnp.bfloat16)
```

```python
import jax
import jax.numpy as jnp
from jax import lax
from jax.experimental import pallas as pl
from jax.experimental.pallas import tpu as pltpu
from jax.sharding import PartitionSpec as P

NBG = 512
BAND = 3
FAR = 160
BS = 128
LAYERS = 4
PAIRS = NBG // 2
FAR_PAIRS = FAR // 2
AXES = ("layer", "row", "col")
OFFSETS = list(range(-BAND, BAND + 1)) + [
    FAR - 1, FAR, FAR + 1, -FAR - 1, -FAR, -FAR + 1,
]
DIAGS = len(OFFSETS)
OFFSET_SET = {value % NBG for value in OFFSETS}

REACH = (
    list(range(-BAND, BAND + 2))
    + list(range(FAR - 1, FAR + 3))
    + list(range(-FAR - 1, -FAR + 3))
)
SLOT = {value % NBG: index for index, value in enumerate(REACH)}
NEAR_END = 8 * BS
PLUS_END = 12 * BS
WIDTH = 16 * BS


def needed(j):
    found = set()
    for i in range(2):
        for left in OFFSETS:
            if (i + left - j) % NBG == 0:
                for b, right in enumerate(OFFSETS):
                    if (left + right) % NBG in OFFSET_SET:
                        found.add(b)
    return sorted(found)


def tiles_of(rows):
    return [
        (t, b)
        for t in range(2)
        for b in sorted(set().union(*(needed(j) for j in rows[t])))
    ]


LOW = (-1, tiles_of(([-2], [-1])))
HIGH = (1, tiles_of(([2], [3])))
LOWER = (-2, tiles_of(([], [-3])))
HIGHER = (2, tiles_of(([4], [])))
PLUS = (FAR_PAIRS, tiles_of(([FAR, FAR + 2], [FAR + 1, FAR - 1])))
MINUS = (-FAR_PAIRS, tiles_of(([-FAR, -FAR + 2], [-FAR + 1, -FAR - 1])))
DIRECT = [PLUS, MINUS, LOW, HIGH, LOWER, HIGHER]
FAR_LOW = [(0, 1, b) for b in needed(FAR - 1)] + [(1, 1, b) for b in needed(-FAR - 1)]
FAR_HIGH = [(0, 0, b) for b in needed(FAR + 2)] + [(1, 0, b) for b in needed(-FAR + 2)]


def place_of(p):
    return p % LAYERS * (PAIRS // LAYERS) + p // LAYERS


def moved(x, source_of):
    route = [(place_of(source_of(p)), place_of(p)) for p in range(PAIRS)]
    return lax.ppermute(x, AXES, route)


def from_pair(x, distance):
    return moved(x, lambda p: (p + distance) % PAIRS)


def from_layer(x, distance):
    return moved(x, lambda p: p - p % LAYERS + (p + distance) % LAYERS)


def bf16(*shape):
    return jax.ShapeDtypeStruct(shape, jnp.bfloat16)


def call(body, out_shape, n_smem, n_vmem, scratch=(), flops=0, traffic=1 << 22):
    in_specs = [pl.BlockSpec(memory_space=pltpu.SMEM)] * n_smem
    in_specs += [pl.BlockSpec(memory_space=pltpu.VMEM)] * n_vmem
    return pl.pallas_call(
        body,
        out_shape=out_shape,
        in_specs=in_specs,
        out_specs=jax.tree.map(
            lambda _: pl.BlockSpec(memory_space=pltpu.VMEM), out_shape
        ),
        scratch_shapes=list(scratch),
        compiler_params=pltpu.CompilerParams(vmem_limit_bytes=48 << 20),
        cost_estimate=pl.CostEstimate(
            flops=flops, bytes_accessed=traffic, transcendentals=0
        ),
    )


def split_body(me_ref, presence_ref, blocks_ref, *out_refs):
    me = me_ref[0]
    for s, out_ref in enumerate(out_refs):
        other = lax.rem(me - s + LAYERS, LAYERS)
        for t in range(2):
            row = 2 * other + t
            for d in range(DIAGS):
                tile = blocks_ref[d, row]
                present = presence_ref[d, row] != 0
                out_ref[d, t] = jnp.where(present, tile, jnp.zeros_like(tile))


def pack_body(me_ref, *refs):
    me = me_ref[0]
    pieces, own_ref, out_refs = refs[:LAYERS], refs[LAYERS], refs[LAYERS + 1 :]
    for s, piece in enumerate(pieces):
        other = lax.rem(me + s, LAYERS)
        start = pl.multiple_of(other * (BS // LAYERS), BS // LAYERS)
        own_ref[:, :, pl.ds(start, BS // LAYERS), :] = piece[...]
    for (_, tiles), out_ref in zip(DIRECT, out_refs):
        for k, (t, b) in enumerate(tiles):
            out_ref[k] = own_ref[b, t]


def far_body(plus_ref, minus_ref, low_ref, high_ref):
    sources = ((plus_ref, PLUS[1]), (minus_ref, MINUS[1]))
    for message, out_ref in ((FAR_LOW, low_ref), (FAR_HIGH, high_ref)):
        for k, (which, t, b) in enumerate(message):
            ref, tiles = sources[which]
            out_ref[k] = ref[tiles.index((t, b))]


def placements():
    found = {}

    def place(operand, index, j, b):
        row, column = SLOT[j % NBG], SLOT[(j + OFFSETS[b]) % NBG]
        found[row, column] = (operand, index)

    for t in range(2):
        for b in range(DIAGS):
            place(0, (b, t), t, b)
    for operand, (distance, tiles) in enumerate(DIRECT):
        for k, (t, b) in enumerate(tiles):
            j = 2 * distance + t
            if b in needed(j):
                place(1 + operand, k, j, b)
    for operand, message, rows in (
        (7, FAR_LOW, (FAR - 1, -FAR - 1)),
        (8, FAR_HIGH, (FAR + 2, -FAR + 2)),
    ):
        for k, (which, t, b) in enumerate(message):
            place(operand, k, rows[which], b)
    return found


def purify_body(me_ref, presence_ref, *refs):
    sources, outs = refs[:9], refs[9:13]
    right_ref, left_ref, result_ref = refs[13:]
    me = me_ref[0]
    own_ref = sources[0]
    placed = placements()
    zero = jnp.zeros((BS, BS), jnp.bfloat16)
    for row in range(16):
        for column in range(16):
            where = (pl.ds(row * BS, BS), pl.ds(column * BS, BS))
            if (row, column) in placed:
                operand, index = placed[row, column]
                right_ref[where] = sources[operand][index]
            else:
                right_ref[where] = zero
    targets = {
        (i, SLOT[(i + offset) % NBG]): d
        for i in range(2)
        for d, offset in enumerate(OFFSETS)
    }
    for i in range(2):
        for column in range(16):
            where = (pl.ds(i * BS, BS), pl.ds(column * BS, BS))
            d = targets.get((i, column))
            left_ref[where] = zero if d is None else own_ref[d, i]

    def dot(left, right):
        return jnp.dot(left, right, preferred_element_type=jnp.float32)

    def product(columns):
        start = columns[0] * BS
        wide = pl.ds(start, len(columns) * BS)
        if start < NEAR_END:
            return dot(left_ref[...], right_ref[:, wide])
        if start < PLUS_END:
            return dot(left_ref[:, :PLUS_END], right_ref[:PLUS_END, wide])
        return dot(left_ref[:, :NEAR_END], right_ref[:NEAR_END, wide]) + dot(
            left_ref[:, PLUS_END:], right_ref[PLUS_END:, wide]
        )

    def each(columns, total, use):
        for at, column in enumerate(columns):
            for i in range(2):
                d = targets.get((i, column))
                if d is not None:
                    tile = total[i * BS : (i + 1) * BS, at * BS : (at + 1) * BS]
                    use(i, column, d, presence_ref[d, 2 * me + i] != 0, tile)

    groups = [[c, c + 1] for c in range(0, 16, 2)]

    def keep_second(i, column, d, present, tile):
        second = jnp.where(present, tile, jnp.zeros_like(tile)).astype(jnp.bfloat16)
        result_ref[d, i] = second

    for columns in groups:
        each(columns, product(columns), keep_second)
    for (i, column), d in targets.items():
        left_ref[pl.ds(i * BS, BS), pl.ds(column * BS, BS)] = result_ref[d, i]

    def keep_result(i, column, d, present, tile):
        third = jnp.where(present, tile, jnp.zeros_like(tile))
        second = result_ref[d, i].astype(jnp.float32)
        result_ref[d, i] = (3.0 * second - 2.0 * third).astype(jnp.bfloat16)

    for columns in groups:
        each(columns, product(columns), keep_result)
    for s, out_ref in enumerate(outs):
        other = lax.rem(me - s + LAYERS, LAYERS)
        start = pl.multiple_of(other * (BS // LAYERS), BS // LAYERS)
        out_ref[...] = result_ref[:, :, pl.ds(start, BS // LAYERS), :]


def join_body(me_ref, *refs):
    me = me_ref[0]
    out_ref = refs[LAYERS]
    for s in range(LAYERS):
        row = 2 * lax.rem(me + s, LAYERS)
        for t in range(2):
            for d in range(DIAGS):
                out_ref[d, row + t] = refs[s][d, t]


def per_device(blocks, presence):
    me = lax.axis_index("layer").astype(jnp.int32).reshape(1)
    quarter = bf16(DIAGS, 2, BS // LAYERS, BS)
    tiles = [bf16(len(message), BS, BS) for _, message in DIRECT]

    pieces = call(split_body, [quarter] * LAYERS, 2, 1)(me, presence, blocks)
    pieces = [pieces[0]] + [from_layer(pieces[s], s) for s in range(1, LAYERS)]
    own, *messages = call(
        pack_body, [bf16(DIAGS, 2, BS, BS)] + tiles, 1, LAYERS
    )(me, *pieces)
    arrived = [
        from_pair(message, distance)
        for message, (distance, _) in zip(messages, DIRECT)
    ]
    far_low, far_high = call(
        far_body, [bf16(len(FAR_LOW), BS, BS), bf16(len(FAR_HIGH), BS, BS)], 0, 2
    )(arrived[0], arrived[1])
    far_low, far_high = from_pair(far_low, -1), from_pair(far_high, 1)
    results = call(
        purify_body,
        [quarter] * LAYERS,
        2,
        9,
        scratch=[
            pltpu.VMEM((WIDTH, WIDTH), jnp.bfloat16),
            pltpu.VMEM((2 * BS, WIDTH), jnp.bfloat16),
            pltpu.VMEM((DIAGS, 2, BS, BS), jnp.bfloat16),
        ],
        flops=4 * 224 * 2 * BS**3,
    )(me, presence, own, *arrived, far_low, far_high)
    results = [results[0]] + [from_layer(results[s], s) for s in range(1, LAYERS)]
    return call(join_body, bf16(DIAGS, 2 * LAYERS, BS // LAYERS, BS), 1, LAYERS)(
        me, *results
    )


def solution(mesh):
    placed = (P(None, ("row", "col"), "layer", None), P(None, ("row", "col")))
    return jax.shard_map(
        per_device,
        mesh=mesh,
        in_specs=placed,
        out_specs=P(None, ("row", "col"), "layer", None),
        check_vma=False,
    )
```

```python
import jax
import jax.numpy as jnp
from jax import lax
from jax.experimental import pallas as pl
from jax.experimental.pallas import tpu as pltpu
from jax.sharding import PartitionSpec as P

NBG = 512
BAND = 3
FAR = 160
BS = 128
LAYERS = 4
PAIRS = NBG // 2
FAR_PAIRS = FAR // 2
AXES = ("layer", "row", "col")
OFFSETS = list(range(-BAND, BAND + 1)) + [
    FAR - 1, FAR, FAR + 1, -FAR - 1, -FAR, -FAR + 1,
]
DIAGS = len(OFFSETS)
OFFSET_SET = {value % NBG for value in OFFSETS}

REACH = (
    list(range(-BAND, BAND + 2))
    + list(range(FAR - 1, FAR + 3))
    + list(range(-FAR - 1, -FAR + 3))
)
SLOT = {value % NBG: index for index, value in enumerate(REACH)}
NEAR_END = 8 * BS
PLUS_END = 12 * BS
WIDTH = 16 * BS


def needed(j):
    found = set()
    for i in range(2):
        for left in OFFSETS:
            if (i + left - j) % NBG == 0:
                for b, right in enumerate(OFFSETS):
                    if (left + right) % NBG in OFFSET_SET:
                        found.add(b)
    return sorted(found)


BANDS = range(2 * BAND + 1)
SHARED = sorted(b for b in set().union(*(needed(FAR + t) for t in range(-1, 3))) if b in BANDS)


def band_of(j):
    return [b for b in needed(j) if b in BANDS]


def far_of(j):
    return [b for b in needed(j) if b not in BANDS]


def tiles(rows, which=needed):
    return [(j, b) for j in rows for b in which(j)]


OWN = [(t, b) for b in range(DIAGS) for t in range(2)]
LOW, HIGH = tiles([-2, -1]), tiles([2, 3])
LOWER, HIGHER = tiles([-3]), tiles([4])
PLUS_BAND = tiles(range(FAR - 1, FAR + 3), band_of)
MINUS_BAND = tiles(range(-FAR - 1, -FAR + 3), band_of)
PLUS_FAR = tiles([FAR, FAR + 1], far_of)
MINUS_FAR = tiles([-FAR, -FAR + 1], far_of)
LOW_FAR = tiles([FAR - 1, -FAR - 1], far_of)
HIGH_FAR = tiles([FAR + 2, -FAR + 2], far_of)
ARRIVE = [
    OWN, LOW, HIGH, LOWER, HIGHER, PLUS_BAND, MINUS_BAND,
    PLUS_FAR, MINUS_FAR, LOW_FAR, HIGH_FAR,
]
assert [(j - FAR, b) for j, b in PLUS_BAND] == [(j + FAR, b) for j, b in MINUS_BAND]
NEAR = [[(j % 2, b) for j, b in message] for message in (LOW, HIGH, LOWER, HIGHER)]
DIRECT = [[(j % 2, b) for j, b in message] for message in (PLUS_FAR, MINUS_FAR)]
EDGE_LOW = [(1, b) for b in band_of(FAR - 1)]
EDGE_HIGH = [(0, b) for b in band_of(FAR + 2)]


def place_of(p):
    return p % LAYERS * (PAIRS // LAYERS) + p // LAYERS


def moved(x, source_of):
    route = [(place_of(source_of(p)), place_of(p)) for p in range(PAIRS)]
    return lax.ppermute(x, AXES, route)


def across(p):
    cols = LAYERS * 8
    return p - p % cols + (p + cols // 2) % cols


def from_pair(x, distance):
    return moved(x, lambda p: (p + distance) % PAIRS)


def same_group(p, distance):
    return p - p % LAYERS + (p + distance) % LAYERS


def from_layer(x, distance):
    return moved(x, lambda p: same_group(p, distance))


def from_layer_across(x, distance):
    return moved(x, lambda p: across(same_group(p, distance)))


def edge_across(x, distance):
    return moved(x, lambda p: across((across(p) + distance) % PAIRS))


def far_across(x, distance):
    return moved(x, lambda p: across((p + distance) % PAIRS))


def bf16(*shape):
    return jax.ShapeDtypeStruct(shape, jnp.bfloat16)


def call(body, out_shape, n_smem, n_vmem, scratch=(), flops=0, traffic=1 << 22):
    in_specs = [pl.BlockSpec(memory_space=pltpu.SMEM)] * n_smem
    in_specs += [pl.BlockSpec(memory_space=pltpu.VMEM)] * n_vmem
    return pl.pallas_call(
        body,
        out_shape=out_shape,
        in_specs=in_specs,
        out_specs=jax.tree.map(
            lambda _: pl.BlockSpec(memory_space=pltpu.VMEM), out_shape
        ),
        scratch_shapes=list(scratch),
        compiler_params=pltpu.CompilerParams(vmem_limit_bytes=48 << 20),
        cost_estimate=pl.CostEstimate(
            flops=flops, bytes_accessed=traffic, transcendentals=0
        ),
    )


def split_body(me_ref, presence_ref, blocks_ref, *out_refs):
    me = me_ref[0]
    for s in range(LAYERS):
        own_ref, shared_ref = out_refs[s], out_refs[LAYERS + s]
        other = lax.rem(me - s + LAYERS, LAYERS)
        for t in range(2):
            row = 2 * other + t
            for d in range(DIAGS):
                tile = blocks_ref[d, row]
                present = presence_ref[d, row] != 0
                tile = jnp.where(present, tile, jnp.zeros_like(tile))
                own_ref[d, t] = tile
                if d in SHARED:
                    shared_ref[SHARED.index(d), t] = tile


def gather_pieces(me, pieces, out_ref):
    for s, piece in enumerate(pieces):
        other = lax.rem(me + s, LAYERS)
        start = pl.multiple_of(other * (BS // LAYERS), BS // LAYERS)
        out_ref[:, :, pl.ds(start, BS // LAYERS), :] = piece[...]


def pack_body(me_ref, *refs):
    pieces, own_ref, out_refs = refs[:LAYERS], refs[LAYERS], refs[LAYERS + 1 :]
    gather_pieces(me_ref[0], pieces, own_ref)
    for message, out_ref in zip(DIRECT + NEAR, out_refs):
        for k, (t, b) in enumerate(message):
            out_ref[k] = own_ref[b, t]


def edge_body(me_ref, *refs):
    pieces, shared_ref, out_refs = refs[:LAYERS], refs[LAYERS], refs[LAYERS + 1 :]
    gather_pieces(me_ref[0], pieces, shared_ref)
    for message, out_ref in zip((EDGE_LOW, EDGE_HIGH), out_refs):
        for k, (t, b) in enumerate(message):
            out_ref[k] = shared_ref[SHARED.index(b), t]


def fan_body(shared_ref, low_ref, high_ref, out_ref):
    for k, (j, b) in enumerate(PLUS_BAND):
        t = j - FAR
        if t < 0:
            out_ref[k] = low_ref[EDGE_LOW.index((1, b))]
        elif t > 1:
            out_ref[k] = high_ref[EDGE_HIGH.index((0, b))]
        else:
            out_ref[k] = shared_ref[SHARED.index(b), t]


def far_body(plus_ref, minus_ref, low_ref, high_ref):
    for shift, message, out_ref in ((2, LOW_FAR, low_ref), (-2, HIGH_FAR, high_ref)):
        for k, (j, b) in enumerate(message):
            if j > 0:
                out_ref[k] = plus_ref[PLUS_FAR.index((j + shift, b))]
            else:
                out_ref[k] = minus_ref[MINUS_FAR.index((j + shift, b))]


def placements():
    found = {}
    for operand, message in enumerate(ARRIVE):
        for k, (j, b) in enumerate(message):
            column = SLOT[(j + OFFSETS[b]) % NBG]
            found[SLOT[j % NBG], column] = (operand, k if operand else (b, j))
    return found


def purify_body(me_ref, presence_ref, *refs):
    sources, outs = refs[: len(ARRIVE)], refs[len(ARRIVE) : len(ARRIVE) + LAYERS]
    right_ref, left_ref, result_ref = refs[len(ARRIVE) + LAYERS :]
    me = me_ref[0]
    own_ref = sources[0]
    placed = placements()
    zero = jnp.zeros((BS, BS), jnp.bfloat16)
    for row in range(16):
        for column in range(16):
            where = (pl.ds(row * BS, BS), pl.ds(column * BS, BS))
            if (row, column) in placed:
                operand, index = placed[row, column]
                right_ref[where] = sources[operand][index]
            else:
                right_ref[where] = zero
    targets = {
        (i, SLOT[(i + offset) % NBG]): d
        for i in range(2)
        for d, offset in enumerate(OFFSETS)
    }
    for i in range(2):
        for column in range(16):
            where = (pl.ds(i * BS, BS), pl.ds(column * BS, BS))
            d = targets.get((i, column))
            left_ref[where] = zero if d is None else own_ref[d, i]

    def dot(left, right):
        return jnp.dot(left, right, preferred_element_type=jnp.float32)

    def product(columns):
        start = columns[0] * BS
        wide = pl.ds(start, len(columns) * BS)
        if start < NEAR_END:
            return dot(left_ref[...], right_ref[:, wide])
        if start < PLUS_END:
            return dot(left_ref[:, :PLUS_END], right_ref[:PLUS_END, wide])
        return dot(left_ref[:, :NEAR_END], right_ref[:NEAR_END, wide]) + dot(
            left_ref[:, PLUS_END:], right_ref[PLUS_END:, wide]
        )

    def each(columns, total, use):
        for at, column in enumerate(columns):
            for i in range(2):
                d = targets.get((i, column))
                if d is not None:
                    tile = total[i * BS : (i + 1) * BS, at * BS : (at + 1) * BS]
                    use(i, column, d, presence_ref[d, 2 * me + i] != 0, tile)

    groups = [[c, c + 1] for c in range(0, 16, 2)]

    def keep_second(i, column, d, present, tile):
        second = jnp.where(present, tile, jnp.zeros_like(tile)).astype(jnp.bfloat16)
        result_ref[d, i] = second

    for columns in groups:
        each(columns, product(columns), keep_second)
    for (i, column), d in targets.items():
        left_ref[pl.ds(i * BS, BS), pl.ds(column * BS, BS)] = result_ref[d, i]

    def keep_result(i, column, d, present, tile):
        third = jnp.where(present, tile, jnp.zeros_like(tile))
        second = result_ref[d, i].astype(jnp.float32)
        result_ref[d, i] = (3.0 * second - 2.0 * third).astype(jnp.bfloat16)

    for columns in groups:
        each(columns, product(columns), keep_result)
    for s, out_ref in enumerate(outs):
        other = lax.rem(me - s + LAYERS, LAYERS)
        start = pl.multiple_of(other * (BS // LAYERS), BS // LAYERS)
        out_ref[...] = result_ref[:, :, pl.ds(start, BS // LAYERS), :]


def join_body(me_ref, *refs):
    me = me_ref[0]
    out_ref = refs[LAYERS]
    for s in range(LAYERS):
        row = 2 * lax.rem(me + s, LAYERS)
        for t in range(2):
            for d in range(DIAGS):
                out_ref[d, row + t] = refs[s][d, t]


def per_device(blocks, presence):
    me = lax.axis_index("layer").astype(jnp.int32).reshape(1)
    quarter = bf16(DIAGS, 2, BS // LAYERS, BS)
    shared_quarter = bf16(len(SHARED), 2, BS // LAYERS, BS)

    def packed(messages):
        return [bf16(len(message), BS, BS) for message in messages]

    pieces = call(split_body, [quarter] * LAYERS + [shared_quarter] * LAYERS, 2, 1)(
        me, presence, blocks
    )
    shared = [from_layer_across(pieces[LAYERS + s], s) for s in range(LAYERS)]
    pieces = [pieces[0]] + [from_layer(pieces[s], s) for s in range(1, LAYERS)]
    shared, edge_low, edge_high = call(
        edge_body,
        [bf16(len(SHARED), 2, BS, BS)] + packed([EDGE_LOW, EDGE_HIGH]),
        1,
        LAYERS,
    )(me, *shared)
    edge_low, edge_high = edge_across(edge_low, -1), edge_across(edge_high, 1)
    own, plus_far, minus_far, low, high, lower, higher = call(
        pack_body, [bf16(DIAGS, 2, BS, BS)] + packed(DIRECT + NEAR), 1, LAYERS
    )(me, *pieces)
    plus_far = from_pair(plus_far, FAR_PAIRS)
    minus_far = from_pair(minus_far, -FAR_PAIRS)
    low, high = from_pair(low, -1), from_pair(high, 1)
    lower, higher = from_pair(lower, -2), from_pair(higher, 2)
    band = call(fan_body, packed([PLUS_BAND])[0], 0, 3)(shared, edge_low, edge_high)
    plus_band, minus_band = far_across(band, FAR_PAIRS), far_across(band, -FAR_PAIRS)
    low_far, high_far = call(far_body, packed([LOW_FAR, HIGH_FAR]), 0, 2)(
        plus_far, minus_far
    )
    low_far, high_far = from_pair(low_far, -1), from_pair(high_far, 1)
    results = call(
        purify_body,
        [quarter] * LAYERS,
        2,
        len(ARRIVE),
        scratch=[
            pltpu.VMEM((WIDTH, WIDTH), jnp.bfloat16),
            pltpu.VMEM((2 * BS, WIDTH), jnp.bfloat16),
            pltpu.VMEM((DIAGS, 2, BS, BS), jnp.bfloat16),
        ],
        flops=4 * 224 * 2 * BS**3,
    )(
        me, presence, own, low, high, lower, higher, plus_band, minus_band,
        plus_far, minus_far, low_far, high_far,
    )
    results = [results[0]] + [from_layer(results[s], s) for s in range(1, LAYERS)]
    return call(join_body, bf16(DIAGS, 2 * LAYERS, BS // LAYERS, BS), 1, LAYERS)(
        me, *results
    )


def solution(mesh):
    placed = (P(None, ("row", "col"), "layer", None), P(None, ("row", "col")))
    return jax.shard_map(
        per_device,
        mesh=mesh,
        in_specs=placed,
        out_specs=P(None, ("row", "col"), "layer", None),
        check_vma=False,
    )
```

```python
import jax
import jax.numpy as jnp
from jax import lax
from jax.experimental import pallas as pl
from jax.experimental.pallas import tpu as pltpu
from jax.sharding import PartitionSpec as P

NBG = 512
BAND = 3
FAR = 160
BS = 128
LAYERS = 4
PAIRS = NBG // 2
FAR_PAIRS = FAR // 2
AXES = ("layer", "row", "col")
OFFSETS = list(range(-BAND, BAND + 1)) + [
    FAR - 1, FAR, FAR + 1, -FAR - 1, -FAR, -FAR + 1,
]
DIAGS = len(OFFSETS)
OFFSET_SET = {value % NBG for value in OFFSETS}

REACH = (
    list(range(-BAND, BAND + 2))
    + list(range(FAR - 1, FAR + 3))
    + list(range(-FAR - 1, -FAR + 3))
)
SLOT = {value % NBG: index for index, value in enumerate(REACH)}
NEAR_END = 8 * BS
PLUS_END = 12 * BS
WIDTH = 16 * BS


def needed(j):
    found = set()
    for i in range(2):
        for left in OFFSETS:
            if (i + left - j) % NBG == 0:
                for b, right in enumerate(OFFSETS):
                    if (left + right) % NBG in OFFSET_SET:
                        found.add(b)
    return sorted(found)


BANDS = range(2 * BAND + 1)
SHARED = sorted(b for b in set().union(*(needed(FAR + t) for t in range(-1, 3))) if b in BANDS)


def band_of(j):
    return [b for b in needed(j) if b in BANDS]


def far_of(j):
    return [b for b in needed(j) if b not in BANDS]


def tiles(rows, which=needed):
    return [(j, b) for j in rows for b in which(j)]


OWN = [(t, b) for b in range(DIAGS) for t in range(2)]
LOW, HIGH = tiles([-2, -1]), tiles([2, 3])
FAN = [(t, b) for t in range(2) for b in SHARED]
PLUS_BAND = [(t + FAR, b) for t, b in FAN]
MINUS_BAND = [(t - FAR, b) for t, b in FAN]
PLUS_FAR = tiles([FAR, FAR + 1], far_of)
MINUS_FAR = tiles([-FAR, -FAR + 1], far_of)
EDGE_LOW = tiles([-3, FAR - 1, -FAR - 1])
EDGE_HIGH = tiles([4, FAR + 2, -FAR + 2])
MAIN = [OWN, LOW, HIGH, PLUS_BAND, MINUS_BAND, PLUS_FAR, MINUS_FAR]
ARRIVE = MAIN + [EDGE_LOW, EDGE_HIGH]
NEAR = [[(j % 2, b) for j, b in message] for message in (LOW, HIGH)]
DIRECT = [[(j % 2, b) for j, b in message] for message in (PLUS_FAR, MINUS_FAR)]


def place_of(p):
    return p % LAYERS * (PAIRS // LAYERS) + p // LAYERS


def moved(x, source_of):
    route = [(place_of(source_of(p)), place_of(p)) for p in range(PAIRS)]
    return lax.ppermute(x, AXES, route)


def across(p):
    cols = LAYERS * 8
    return p - p % cols + (p + cols // 2) % cols


def from_pair(x, distance):
    return moved(x, lambda p: (p + distance) % PAIRS)


def same_group(p, distance):
    return p - p % LAYERS + (p + distance) % LAYERS


def from_layer(x, distance):
    return moved(x, lambda p: same_group(p, distance))


def from_layer_across(x, distance):
    return moved(x, lambda p: across(same_group(p, distance)))


def far_across(x, distance):
    return moved(x, lambda p: across((p + distance) % PAIRS))


def bf16(*shape):
    return jax.ShapeDtypeStruct(shape, jnp.bfloat16)


def call(body, out_shape, n_smem, n_vmem, scratch=(), flops=0, traffic=1 << 22):
    in_specs = [pl.BlockSpec(memory_space=pltpu.SMEM)] * n_smem
    in_specs += [pl.BlockSpec(memory_space=pltpu.VMEM)] * n_vmem
    return pl.pallas_call(
        body,
        out_shape=out_shape,
        in_specs=in_specs,
        out_specs=jax.tree.map(
            lambda _: pl.BlockSpec(memory_space=pltpu.VMEM), out_shape
        ),
        scratch_shapes=list(scratch),
        compiler_params=pltpu.CompilerParams(vmem_limit_bytes=48 << 20),
        cost_estimate=pl.CostEstimate(
            flops=flops, bytes_accessed=traffic, transcendentals=0
        ),
    )


def split_body(me_ref, presence_ref, blocks_ref, *out_refs):
    me = me_ref[0]
    for s in range(LAYERS):
        own_ref, shared_ref = out_refs[s], out_refs[LAYERS + s]
        other = lax.rem(me - s + LAYERS, LAYERS)
        for t in range(2):
            row = 2 * other + t
            for d in range(DIAGS):
                tile = blocks_ref[d, row]
                present = presence_ref[d, row] != 0
                tile = jnp.where(present, tile, jnp.zeros_like(tile))
                own_ref[d, t] = tile
                if d in SHARED:
                    shared_ref[SHARED.index(d), t] = tile


def gather_pieces(me, pieces, out_ref):
    for s, piece in enumerate(pieces):
        other = lax.rem(me + s, LAYERS)
        start = pl.multiple_of(other * (BS // LAYERS), BS // LAYERS)
        out_ref[:, :, pl.ds(start, BS // LAYERS), :] = piece[...]


def pack_body(me_ref, *refs):
    pieces, own_ref, out_refs = refs[:LAYERS], refs[LAYERS], refs[LAYERS + 1 :]
    gather_pieces(me_ref[0], pieces, own_ref)
    for message, out_ref in zip(DIRECT, out_refs):
        for k, (t, b) in enumerate(message):
            out_ref[k] = own_ref[b, t]


def near_body(own_ref, after_ref, *out_refs):
    del after_ref
    for message, out_ref in zip(NEAR, out_refs):
        for k, (t, b) in enumerate(message):
            out_ref[k] = own_ref[b, t]


def fan_body(me_ref, *refs):
    pieces, out_ref, shared_ref = refs[:LAYERS], refs[LAYERS], refs[LAYERS + 1]
    gather_pieces(me_ref[0], pieces, shared_ref)
    for k, (t, b) in enumerate(FAN):
        out_ref[k] = shared_ref[SHARED.index(b), t]


def edge_body(*refs):
    sources, out_refs = refs[: len(MAIN) - 1], refs[len(MAIN) - 1 :]
    for shift, message, out_ref in zip((2, -2), (EDGE_LOW, EDGE_HIGH), out_refs):
        for k, (j, b) in enumerate(message):
            [(ref, held)] = [
                (ref, held)
                for ref, held in zip(sources, MAIN[1:])
                if (j + shift, b) in held
            ]
            out_ref[k] = ref[held.index((j + shift, b))]


def placements():
    found = {}
    for operand, message in enumerate(ARRIVE):
        for k, (j, b) in enumerate(message):
            column = SLOT.get((j + OFFSETS[b]) % NBG)
            if column is not None:
                found[SLOT[j % NBG], column] = (operand, k if operand else (b, j))
    return found


def purify_body(me_ref, presence_ref, *refs):
    sources, outs = refs[: len(ARRIVE)], refs[len(ARRIVE) : len(ARRIVE) + LAYERS]
    right_ref, left_ref, result_ref = refs[len(ARRIVE) + LAYERS :]
    me = me_ref[0]
    own_ref = sources[0]
    placed = placements()
    zero = jnp.zeros((BS, BS), jnp.bfloat16)
    for row in range(16):
        for column in range(16):
            where = (pl.ds(row * BS, BS), pl.ds(column * BS, BS))
            if (row, column) in placed:
                operand, index = placed[row, column]
                right_ref[where] = sources[operand][index]
            else:
                right_ref[where] = zero
    targets = {
        (i, SLOT[(i + offset) % NBG]): d
        for i in range(2)
        for d, offset in enumerate(OFFSETS)
    }
    for i in range(2):
        for column in range(16):
            where = (pl.ds(i * BS, BS), pl.ds(column * BS, BS))
            d = targets.get((i, column))
            left_ref[where] = zero if d is None else own_ref[d, i]

    def dot(left, right):
        return jnp.dot(left, right, preferred_element_type=jnp.float32)

    def product(columns):
        start = columns[0] * BS
        wide = pl.ds(start, len(columns) * BS)
        if start < NEAR_END:
            return dot(left_ref[...], right_ref[:, wide])
        if start < PLUS_END:
            return dot(left_ref[:, :PLUS_END], right_ref[:PLUS_END, wide])
        return dot(left_ref[:, :NEAR_END], right_ref[:NEAR_END, wide]) + dot(
            left_ref[:, PLUS_END:], right_ref[PLUS_END:, wide]
        )

    def each(columns, total, use):
        for at, column in enumerate(columns):
            for i in range(2):
                d = targets.get((i, column))
                if d is not None:
                    tile = total[i * BS : (i + 1) * BS, at * BS : (at + 1) * BS]
                    use(i, column, d, presence_ref[d, 2 * me + i] != 0, tile)

    groups = [[c, c + 1] for c in range(0, 16, 2)]

    def keep_second(i, column, d, present, tile):
        second = jnp.where(present, tile, jnp.zeros_like(tile)).astype(jnp.bfloat16)
        result_ref[d, i] = second

    for columns in groups:
        each(columns, product(columns), keep_second)
    for (i, column), d in targets.items():
        left_ref[pl.ds(i * BS, BS), pl.ds(column * BS, BS)] = result_ref[d, i]

    def keep_result(i, column, d, present, tile):
        third = jnp.where(present, tile, jnp.zeros_like(tile))
        second = result_ref[d, i].astype(jnp.float32)
        result_ref[d, i] = (3.0 * second - 2.0 * third).astype(jnp.bfloat16)

    for columns in groups:
        each(columns, product(columns), keep_result)
    for s, out_ref in enumerate(outs):
        other = lax.rem(me - s + LAYERS, LAYERS)
        start = pl.multiple_of(other * (BS // LAYERS), BS // LAYERS)
        out_ref[...] = result_ref[:, :, pl.ds(start, BS // LAYERS), :]


def join_body(me_ref, *refs):
    me = me_ref[0]
    out_ref = refs[LAYERS]
    for s in range(LAYERS):
        row = 2 * lax.rem(me + s, LAYERS)
        for t in range(2):
            for d in range(DIAGS):
                out_ref[d, row + t] = refs[s][d, t]


def per_device(blocks, presence):
    me = lax.axis_index("layer").astype(jnp.int32).reshape(1)
    quarter = bf16(DIAGS, 2, BS // LAYERS, BS)
    shared_quarter = bf16(len(SHARED), 2, BS // LAYERS, BS)

    def packed(messages):
        return [bf16(len(message), BS, BS) for message in messages]

    pieces = call(split_body, [quarter] * LAYERS + [shared_quarter] * LAYERS, 2, 1)(
        me, presence, blocks
    )
    shared = [from_layer_across(pieces[LAYERS + s], s) for s in range(LAYERS)]
    pieces = [pieces[0]] + [from_layer(pieces[s], s) for s in range(1, LAYERS)]
    band = call(
        fan_body,
        packed([FAN])[0],
        1,
        LAYERS,
        scratch=[pltpu.VMEM((len(SHARED), 2, BS, BS), jnp.bfloat16)],
    )(me, *shared)
    own, plus_far, minus_far = call(
        pack_body, [bf16(DIAGS, 2, BS, BS)] + packed(DIRECT), 1, LAYERS
    )(me, *pieces)
    plus_far = from_pair(plus_far, FAR_PAIRS)
    minus_far = from_pair(minus_far, -FAR_PAIRS)
    plus_band, minus_band = far_across(band, FAR_PAIRS), far_across(band, -FAR_PAIRS)
    low, high = call(near_body, packed([LOW, HIGH]), 0, 2)(own, band)
    low, high = from_pair(low, -1), from_pair(high, 1)
    arrived = [low, high, plus_band, minus_band, plus_far, minus_far]
    edge_low, edge_high = call(
        edge_body, packed([EDGE_LOW, EDGE_HIGH]), 0, len(arrived)
    )(*arrived)
    edge_low, edge_high = from_pair(edge_low, -1), from_pair(edge_high, 1)
    results = call(
        purify_body,
        [quarter] * LAYERS,
        2,
        len(ARRIVE),
        scratch=[
            pltpu.VMEM((WIDTH, WIDTH), jnp.bfloat16),
            pltpu.VMEM((2 * BS, WIDTH), jnp.bfloat16),
            pltpu.VMEM((DIAGS, 2, BS, BS), jnp.bfloat16),
        ],
        flops=4 * 224 * 2 * BS**3,
    )(me, presence, own, *arrived, edge_low, edge_high)
    results = [results[0]] + [from_layer(results[s], s) for s in range(1, LAYERS)]
    return call(join_body, bf16(DIAGS, 2 * LAYERS, BS // LAYERS, BS), 1, LAYERS)(
        me, *results
    )


def solution(mesh):
    placed = (P(None, ("row", "col"), "layer", None), P(None, ("row", "col")))
    return jax.shard_map(
        per_device,
        mesh=mesh,
        in_specs=placed,
        out_specs=P(None, ("row", "col"), "layer", None),
        check_vma=False,
    )
```

```python
import functools

import jax
import jax.numpy as jnp
from jax import lax
from jax.experimental import pallas as pl
from jax.experimental.pallas import tpu as pltpu
from jax.sharding import PartitionSpec as P

NBG = 512
BAND = 3
FAR = 160
BS = 128
LAYERS = 4
PAIRS = NBG // 2
FAR_PAIRS = FAR // 2
AXES = ("layer", "row", "col")
OFFSETS = list(range(-BAND, BAND + 1)) + [
    FAR - 1, FAR, FAR + 1, -FAR - 1, -FAR, -FAR + 1,
]
DIAGS = len(OFFSETS)
OFFSET_SET = {value % NBG for value in OFFSETS}

REACH = (
    list(range(-BAND, BAND + 2))
    + list(range(FAR - 1, FAR + 3))
    + list(range(-FAR - 1, -FAR + 3))
)
SLOT = {value % NBG: index for index, value in enumerate(REACH)}
NEAR_END = 8 * BS
PLUS_END = 12 * BS
WIDTH = 16 * BS


def needed(j):
    found = set()
    for i in range(2):
        for left in OFFSETS:
            if (i + left - j) % NBG == 0:
                for b, right in enumerate(OFFSETS):
                    if (left + right) % NBG in OFFSET_SET:
                        found.add(b)
    return sorted(found)


BANDS = range(2 * BAND + 1)
SHARED = sorted(b for b in set().union(*(needed(FAR + t) for t in range(-1, 3))) if b in BANDS)


def band_of(j):
    return [b for b in needed(j) if b in BANDS]


def far_of(j):
    return [b for b in needed(j) if b not in BANDS]


def tiles(rows, which=needed):
    return [(j, b) for j in rows for b in which(j)]


PARTS = [list(range(DIAGS))]

OWN = [[(t, b) for b in part for t in range(2)] for part in PARTS]
LOW, HIGH = tiles([-2, -1]), tiles([2, 3])
FAN = [(t, b) for t in range(2) for b in SHARED]
PLUS_BAND = [(t + FAR, b) for t, b in FAN]
MINUS_BAND = [(t - FAR, b) for t, b in FAN]
PLUS_FAR = tiles([FAR, FAR + 1], far_of)
MINUS_FAR = tiles([-FAR, -FAR + 1], far_of)
EDGE_LOW = tiles([-3, FAR - 1, -FAR - 1])
EDGE_HIGH = tiles([4, FAR + 2, -FAR + 2])
MAIN = [LOW, HIGH, PLUS_BAND, MINUS_BAND, PLUS_FAR, MINUS_FAR]
ARRIVE = OWN + MAIN + [EDGE_LOW, EDGE_HIGH]
NEAR = [[(j % 2, b) for j, b in message] for message in (LOW, HIGH)]
DIRECT = [[(j % 2, b) for j, b in message] for message in (PLUS_FAR, MINUS_FAR)]


def made_in(message):
    [index] = [k for k, part in enumerate(PARTS) if {b for _, b in message} <= set(part)]
    return index


def place_of(p):
    return p % LAYERS * (PAIRS // LAYERS) + p // LAYERS


def moved(x, source_of):
    route = [(place_of(source_of(p)), place_of(p)) for p in range(PAIRS)]
    return lax.ppermute(x, AXES, route)


def across(p):
    cols = LAYERS * 8
    return p - p % cols + (p + cols // 2) % cols


def from_pair(x, distance):
    return moved(x, lambda p: (p + distance) % PAIRS)


def same_group(p, distance):
    return p - p % LAYERS + (p + distance) % LAYERS


def from_layer(x, distance):
    return moved(x, lambda p: same_group(p, distance))


def swapped(x):
    return moved(x, across)


def far_across(x, distance):
    return moved(x, lambda p: across((p + distance) % PAIRS))


def bf16(*shape):
    return jax.ShapeDtypeStruct(shape, jnp.bfloat16)


def call(body, out_shape, n_smem, n_vmem, scratch=(), flops=0, traffic=1 << 22):
    in_specs = [pl.BlockSpec(memory_space=pltpu.SMEM)] * n_smem
    in_specs += [pl.BlockSpec(memory_space=pltpu.VMEM)] * n_vmem
    return pl.pallas_call(
        body,
        out_shape=out_shape,
        in_specs=in_specs,
        out_specs=jax.tree.map(
            lambda _: pl.BlockSpec(memory_space=pltpu.VMEM), out_shape
        ),
        scratch_shapes=list(scratch),
        compiler_params=pltpu.CompilerParams(vmem_limit_bytes=48 << 20),
        cost_estimate=pl.CostEstimate(
            flops=flops, bytes_accessed=traffic, transcendentals=0
        ),
    )


def split_body(me_ref, presence_ref, blocks_ref, *out_refs):
    me = me_ref[0]
    for index, out_ref in enumerate(out_refs):
        part, s = divmod(index, LAYERS)
        other = lax.rem(me - s + LAYERS, LAYERS)
        for t in range(2):
            row = 2 * other + t
            for k, d in enumerate(PARTS[part]):
                tile = blocks_ref[d, row]
                present = presence_ref[d, row] != 0
                out_ref[k, t] = jnp.where(present, tile, jnp.zeros_like(tile))


def gather_body(part, messages, me_ref, *refs):
    pieces, own_ref, out_refs = refs[:LAYERS], refs[LAYERS], refs[LAYERS + 1 :]
    for s, piece in enumerate(pieces):
        other = lax.rem(me_ref[0] + s, LAYERS)
        start = pl.multiple_of(other * (BS // LAYERS), BS // LAYERS)
        own_ref[:, :, pl.ds(start, BS // LAYERS), :] = piece[...]
    for message, out_ref in zip(messages, out_refs):
        for k, (t, b) in enumerate(message):
            out_ref[k] = own_ref[part.index(b), t]


def near_body(*refs):
    own_refs, out_refs = refs[: len(PARTS)], refs[len(PARTS) :]
    for message, out_ref in zip(NEAR, out_refs):
        for k, (t, b) in enumerate(message):
            [(part, ref)] = [(p, r) for p, r in zip(PARTS, own_refs) if b in p]
            out_ref[k] = ref[part.index(b), t]


def fan_body(low_ref, high_ref, band_ref, out_ref):
    del low_ref, high_ref
    out_ref[...] = band_ref[...]


def edge_body(*refs):
    sources, out_refs = refs[: len(MAIN)], refs[len(MAIN) :]
    for shift, message, out_ref in zip((2, -2), (EDGE_LOW, EDGE_HIGH), out_refs):
        for k, (j, b) in enumerate(message):
            [(ref, held)] = [
                (ref, held)
                for ref, held in zip(sources, MAIN)
                if (j + shift, b) in held
            ]
            out_ref[k] = ref[held.index((j + shift, b))]


def placements():
    found = {}
    for operand, message in enumerate(ARRIVE):
        for k, (j, b) in enumerate(message):
            column = SLOT.get((j + OFFSETS[b]) % NBG)
            if column is not None:
                found[SLOT[j % NBG], column] = (operand, divmod(k, 2) if operand < len(OWN) else k)
    return found


def purify_body(me_ref, presence_ref, *refs):
    sources, outs = refs[: len(ARRIVE)], refs[len(ARRIVE) : len(ARRIVE) + LAYERS]
    right_ref, left_ref, result_ref = refs[len(ARRIVE) + LAYERS :]
    me = me_ref[0]
    placed = placements()
    zero = jnp.zeros((BS, BS), jnp.bfloat16)
    for row in range(16):
        for column in range(16):
            where = (pl.ds(row * BS, BS), pl.ds(column * BS, BS))
            if (row, column) in placed:
                operand, index = placed[row, column]
                right_ref[where] = sources[operand][index]
            else:
                right_ref[where] = zero
    targets = {
        (i, SLOT[(i + offset) % NBG]): d
        for i in range(2)
        for d, offset in enumerate(OFFSETS)
    }
    for i in range(2):
        for column in range(16):
            where = (pl.ds(i * BS, BS), pl.ds(column * BS, BS))
            d = targets.get((i, column))
            if d is None:
                left_ref[where] = zero
            else:
                [part] = [p for p, held in enumerate(PARTS) if d in held]
                left_ref[where] = sources[part][PARTS[part].index(d), i]

    def dot(left, right):
        return jnp.dot(left, right, preferred_element_type=jnp.float32)

    def product(columns):
        start = columns[0] * BS
        wide = pl.ds(start, len(columns) * BS)
        if start < NEAR_END:
            return dot(left_ref[...], right_ref[:, wide])
        if start < PLUS_END:
            return dot(left_ref[:, :PLUS_END], right_ref[:PLUS_END, wide])
        return dot(left_ref[:, :NEAR_END], right_ref[:NEAR_END, wide]) + dot(
            left_ref[:, PLUS_END:], right_ref[PLUS_END:, wide]
        )

    def each(columns, total, use):
        for at, column in enumerate(columns):
            for i in range(2):
                d = targets.get((i, column))
                if d is not None:
                    tile = total[i * BS : (i + 1) * BS, at * BS : (at + 1) * BS]
                    use(i, column, d, presence_ref[d, 2 * me + i] != 0, tile)

    groups = [[c, c + 1] for c in range(0, 16, 2)]

    def keep_second(i, column, d, present, tile):
        second = jnp.where(present, tile, jnp.zeros_like(tile)).astype(jnp.bfloat16)
        result_ref[d, i] = second

    for columns in groups:
        each(columns, product(columns), keep_second)
    for (i, column), d in targets.items():
        left_ref[pl.ds(i * BS, BS), pl.ds(column * BS, BS)] = result_ref[d, i]

    def keep_result(i, column, d, present, tile):
        third = jnp.where(present, tile, jnp.zeros_like(tile))
        second = result_ref[d, i].astype(jnp.float32)
        result_ref[d, i] = (3.0 * second - 2.0 * third).astype(jnp.bfloat16)

    for columns in groups:
        each(columns, product(columns), keep_result)
    for s, out_ref in enumerate(outs):
        other = lax.rem(me - s + LAYERS, LAYERS)
        start = pl.multiple_of(other * (BS // LAYERS), BS // LAYERS)
        out_ref[...] = result_ref[:, :, pl.ds(start, BS // LAYERS), :]


def join_body(me_ref, *refs):
    me = me_ref[0]
    out_ref = refs[LAYERS]
    for s in range(LAYERS):
        row = 2 * lax.rem(me + s, LAYERS)
        for t in range(2):
            for d in range(DIAGS):
                out_ref[d, row + t] = refs[s][d, t]


def per_device(blocks, presence):
    me = lax.axis_index("layer").astype(jnp.int32).reshape(1)
    quarter = bf16(DIAGS, 2, BS // LAYERS, BS)

    def packed(messages):
        return [bf16(len(message), BS, BS) for message in messages]

    pieces = call(
        split_body,
        [bf16(len(part), 2, BS // LAYERS, BS) for part in PARTS for _ in range(LAYERS)],
        2,
        1,
    )(me, presence, blocks)
    own, made = [], []
    for index, part in enumerate(PARTS):
        some = pieces[LAYERS * index : LAYERS * (index + 1)]
        some = [some[0]] + [from_layer(some[s], s) for s in range(1, LAYERS)]
        messages = [m for m in [FAN] + DIRECT if made_in(m) == index]
        whole, *outs = call(
            functools.partial(gather_body, part, messages),
            [bf16(len(part), 2, BS, BS)] + packed(messages),
            1,
            LAYERS,
        )(me, *some)
        own.append(whole)
        made += outs
    band, plus_far, minus_far = made
    band = swapped(band)
    plus_far = from_pair(plus_far, FAR_PAIRS)
    minus_far = from_pair(minus_far, -FAR_PAIRS)
    low, high = call(near_body, packed([LOW, HIGH]), 0, len(own))(*own)
    low, high = from_pair(low, -1), from_pair(high, 1)
    band = call(fan_body, packed([FAN])[0], 0, 3)(low, high, band)
    plus_band, minus_band = far_across(band, FAR_PAIRS), far_across(band, -FAR_PAIRS)
    arrived = [low, high, plus_band, minus_band, plus_far, minus_far]
    edge_low, edge_high = call(
        edge_body, packed([EDGE_LOW, EDGE_HIGH]), 0, len(arrived)
    )(*arrived)
    edge_low, edge_high = from_pair(edge_low, -1), from_pair(edge_high, 1)
    results = call(
        purify_body,
        [quarter] * LAYERS,
        2,
        len(ARRIVE),
        scratch=[
            pltpu.VMEM((WIDTH, WIDTH), jnp.bfloat16),
            pltpu.VMEM((2 * BS, WIDTH), jnp.bfloat16),
            pltpu.VMEM((DIAGS, 2, BS, BS), jnp.bfloat16),
        ],
        flops=4 * 224 * 2 * BS**3,
    )(me, presence, *own, *arrived, edge_low, edge_high)
    results = [results[0]] + [from_layer(results[s], s) for s in range(1, LAYERS)]
    return call(join_body, bf16(DIAGS, 2 * LAYERS, BS // LAYERS, BS), 1, LAYERS)(
        me, *results
    )


def solution(mesh):
    placed = (P(None, ("row", "col"), "layer", None), P(None, ("row", "col")))
    return jax.shard_map(
        per_device,
        mesh=mesh,
        in_specs=placed,
        out_specs=P(None, ("row", "col"), "layer", None),
        check_vma=False,
    )
```

```python
import functools

import jax
import jax.numpy as jnp
from jax import lax
from jax.experimental import pallas as pl
from jax.experimental.pallas import tpu as pltpu
from jax.sharding import PartitionSpec as P

NBG = 512
BAND = 3
FAR = 160
BS = 128
LAYERS = 4
PAIRS = NBG // 2
FAR_PAIRS = FAR // 2
AXES = ("layer", "row", "col")
OFFSETS = list(range(-BAND, BAND + 1)) + [
    FAR - 1, FAR, FAR + 1, -FAR - 1, -FAR, -FAR + 1,
]
DIAGS = len(OFFSETS)
OFFSET_SET = {value % NBG for value in OFFSETS}

REACH = (
    list(range(-BAND, BAND + 2))
    + list(range(FAR - 1, FAR + 3))
    + list(range(-FAR - 1, -FAR + 3))
)
SLOT = {value % NBG: index for index, value in enumerate(REACH)}
NEAR_END = 8 * BS
PLUS_END = 12 * BS
WIDTH = 16 * BS


def needed(j):
    found = set()
    for i in range(2):
        for left in OFFSETS:
            if (i + left - j) % NBG == 0:
                for b, right in enumerate(OFFSETS):
                    if (left + right) % NBG in OFFSET_SET:
                        found.add(b)
    return sorted(found)


BANDS = range(2 * BAND + 1)
SHARED = sorted(b for b in set().union(*(needed(FAR + t) for t in range(-1, 3))) if b in BANDS)


def band_of(j):
    return [b for b in needed(j) if b in BANDS]


def far_of(j):
    return [b for b in needed(j) if b not in BANDS]


def tiles(rows, which=needed):
    return [(j, b) for j in rows for b in which(j)]


OWN = [(t, b) for b in range(DIAGS) for t in range(2)]
LOW, HIGH = tiles([-2, -1]), tiles([2, 3])
FAN = tiles(range(FAR - 1, FAR + 3), band_of)
PLUS_BAND = FAN
MINUS_BAND = [(j - 2 * FAR, b) for j, b in FAN]
PLUS_FAR = tiles([FAR, FAR + 1], far_of)
MINUS_FAR = tiles([-FAR, -FAR + 1], far_of)
EDGE_LOW = tiles([-3]) + tiles([FAR - 1, -FAR - 1], far_of)
EDGE_HIGH = tiles([4]) + tiles([FAR + 2, -FAR + 2], far_of)
MAIN = [LOW, HIGH, PLUS_FAR, MINUS_FAR]
ARRIVE = [OWN] + MAIN + [PLUS_BAND, MINUS_BAND, EDGE_LOW, EDGE_HIGH]
NEAR = [[(j % 2, b) for j, b in message] for message in (LOW, HIGH)]
SWAP_LOW = [(1, b) for b in band_of(FAR - 1)]
SWAP_HIGH = [(0, b) for b in band_of(FAR + 2)]
DIRECT = [[(j % 2, b) for j, b in message] for message in (PLUS_FAR, MINUS_FAR)]


def place_of(p):
    return p % LAYERS * (PAIRS // LAYERS) + p // LAYERS


def moved(x, source_of):
    route = [(place_of(source_of(p)), place_of(p)) for p in range(PAIRS)]
    return lax.ppermute(x, AXES, route)


def across(p):
    cols = LAYERS * 8
    return p - p % cols + (p + cols // 2) % cols


def from_pair(x, distance):
    return moved(x, lambda p: (p + distance) % PAIRS)


def same_group(p, distance):
    return p - p % LAYERS + (p + distance) % LAYERS


def from_layer(x, distance):
    return moved(x, lambda p: same_group(p, distance))


def swapped(x):
    return moved(x, across)


def edge_across(x, distance):
    return moved(x, lambda p: across((across(p) + distance) % PAIRS))


def far_across(x, distance):
    return moved(x, lambda p: across((p + distance) % PAIRS))


def bf16(*shape):
    return jax.ShapeDtypeStruct(shape, jnp.bfloat16)


def call(body, out_shape, n_smem, n_vmem, scratch=(), flops=0, traffic=1 << 22):
    in_specs = [pl.BlockSpec(memory_space=pltpu.SMEM)] * n_smem
    in_specs += [pl.BlockSpec(memory_space=pltpu.VMEM)] * n_vmem
    return pl.pallas_call(
        body,
        out_shape=out_shape,
        in_specs=in_specs,
        out_specs=jax.tree.map(
            lambda _: pl.BlockSpec(memory_space=pltpu.VMEM), out_shape
        ),
        scratch_shapes=list(scratch),
        compiler_params=pltpu.CompilerParams(vmem_limit_bytes=48 << 20),
        cost_estimate=pl.CostEstimate(
            flops=flops, bytes_accessed=traffic, transcendentals=0
        ),
    )


def split_body(me_ref, presence_ref, blocks_ref, *out_refs):
    me = me_ref[0]
    shared_ref = out_refs[LAYERS]
    for s in range(LAYERS):
        other = lax.rem(me - s + LAYERS, LAYERS)
        for t in range(2):
            row = 2 * other + t
            for d in range(DIAGS):
                tile = blocks_ref[d, row]
                present = presence_ref[d, row] != 0
                tile = jnp.where(present, tile, jnp.zeros_like(tile))
                out_refs[s][d, t] = tile
                if d in SHARED:
                    shared_ref[SHARED.index(d), row] = tile


def resplit_body(me_ref, shared_ref, *out_refs):
    for s, out_ref in enumerate(out_refs[-LAYERS:]):
        row = 2 * lax.rem(me_ref[0] - s + LAYERS, LAYERS)
        for t in range(2):
            for k in range(len(SHARED)):
                out_ref[k, t] = shared_ref[k, row + t]


def gather_pieces(me, pieces, out_ref):
    for s, piece in enumerate(pieces):
        other = lax.rem(me + s, LAYERS)
        start = pl.multiple_of(other * (BS // LAYERS), BS // LAYERS)
        out_ref[:, :, pl.ds(start, BS // LAYERS), :] = piece[...]


def pack_body(messages, me_ref, *refs):
    pieces, own_ref, out_refs = refs[:LAYERS], refs[LAYERS], refs[LAYERS + 1 :]
    gather_pieces(me_ref[0], pieces, own_ref)
    for message, out_ref in zip(messages, out_refs):
        for k, (t, b) in enumerate(message):
            out_ref[k] = own_ref[b, t]


def near_body(own_ref, *refs):
    for message, out_ref in zip(NEAR, refs[-2:]):
        for k, (t, b) in enumerate(message):
            out_ref[k] = own_ref[b, t]


def shared_body(me_ref, *refs):
    pieces, shared_ref, out_refs = refs[:LAYERS], refs[LAYERS], refs[LAYERS + 1 :]
    gather_pieces(me_ref[0], pieces, shared_ref)
    for message, out_ref in zip((SWAP_LOW, SWAP_HIGH), out_refs):
        for k, (t, b) in enumerate(message):
            out_ref[k] = shared_ref[SHARED.index(b), t]


def fan_body(shared_ref, low_ref, high_ref, *refs):
    out_ref = refs[-1]
    for k, (j, b) in enumerate(FAN):
        t = j - FAR
        if t < 0:
            out_ref[k] = low_ref[SWAP_LOW.index((1, b))]
        elif t > 1:
            out_ref[k] = high_ref[SWAP_HIGH.index((0, b))]
        else:
            out_ref[k] = shared_ref[SHARED.index(b), t]


def edge_body(*refs):
    sources, out_refs = refs[: len(MAIN)], refs[len(MAIN) :]
    for shift, message, out_ref in zip((2, -2), (EDGE_LOW, EDGE_HIGH), out_refs):
        for k, (j, b) in enumerate(message):
            [(ref, held)] = [
                (ref, held)
                for ref, held in zip(sources, MAIN)
                if (j + shift, b) in held
            ]
            out_ref[k] = ref[held.index((j + shift, b))]


def placements():
    found = {}
    for operand, message in enumerate(ARRIVE):
        for k, (j, b) in enumerate(message):
            column = SLOT.get((j + OFFSETS[b]) % NBG)
            if column is not None:
                found[SLOT[j % NBG], column] = (operand, k if operand else (b, j))
    return found


def purify_body(me_ref, presence_ref, *refs):
    sources, outs = refs[: len(ARRIVE)], refs[len(ARRIVE) : len(ARRIVE) + LAYERS]
    right_ref, left_ref, result_ref = refs[len(ARRIVE) + LAYERS :]
    me = me_ref[0]
    placed = placements()
    zero = jnp.zeros((BS, BS), jnp.bfloat16)
    for row in range(16):
        for column in range(16):
            where = (pl.ds(row * BS, BS), pl.ds(column * BS, BS))
            if (row, column) in placed:
                operand, index = placed[row, column]
                right_ref[where] = sources[operand][index]
            else:
                right_ref[where] = zero
    targets = {
        (i, SLOT[(i + offset) % NBG]): d
        for i in range(2)
        for d, offset in enumerate(OFFSETS)
    }
    for i in range(2):
        for column in range(16):
            where = (pl.ds(i * BS, BS), pl.ds(column * BS, BS))
            d = targets.get((i, column))
            left_ref[where] = zero if d is None else sources[0][d, i]

    def dot(left, right):
        return jnp.dot(left, right, preferred_element_type=jnp.float32)

    def product(columns):
        start = columns[0] * BS
        wide = pl.ds(start, len(columns) * BS)
        if start < NEAR_END:
            return dot(left_ref[...], right_ref[:, wide])
        if start < PLUS_END:
            return dot(left_ref[:, :PLUS_END], right_ref[:PLUS_END, wide])
        return dot(left_ref[:, :NEAR_END], right_ref[:NEAR_END, wide]) + dot(
            left_ref[:, PLUS_END:], right_ref[PLUS_END:, wide]
        )

    def each(columns, total, use):
        for at, column in enumerate(columns):
            for i in range(2):
                d = targets.get((i, column))
                if d is not None:
                    tile = total[i * BS : (i + 1) * BS, at * BS : (at + 1) * BS]
                    use(i, column, d, presence_ref[d, 2 * me + i] != 0, tile)

    groups = [[c, c + 1] for c in range(0, 16, 2)]

    def keep_second(i, column, d, present, tile):
        second = jnp.where(present, tile, jnp.zeros_like(tile)).astype(jnp.bfloat16)
        result_ref[d, i] = second

    for columns in groups:
        each(columns, product(columns), keep_second)
    for (i, column), d in targets.items():
        left_ref[pl.ds(i * BS, BS), pl.ds(column * BS, BS)] = result_ref[d, i]

    def keep_result(i, column, d, present, tile):
        third = jnp.where(present, tile, jnp.zeros_like(tile))
        second = result_ref[d, i].astype(jnp.float32)
        result_ref[d, i] = (3.0 * second - 2.0 * third).astype(jnp.bfloat16)

    for columns in groups:
        each(columns, product(columns), keep_result)
    for s, out_ref in enumerate(outs):
        other = lax.rem(me - s + LAYERS, LAYERS)
        start = pl.multiple_of(other * (BS // LAYERS), BS // LAYERS)
        out_ref[...] = result_ref[:, :, pl.ds(start, BS // LAYERS), :]


def join_body(me_ref, *refs):
    me = me_ref[0]
    out_ref = refs[LAYERS]
    for s in range(LAYERS):
        row = 2 * lax.rem(me + s, LAYERS)
        for t in range(2):
            for d in range(DIAGS):
                out_ref[d, row + t] = refs[s][d, t]


def exchanged(pieces):
    far = from_layer(pieces[2], 2)
    return [pieces[0], from_layer(pieces[1], 1), far, from_layer(pieces[3], 3)]


def per_device(blocks, presence):
    me = lax.axis_index("layer").astype(jnp.int32).reshape(1)

    def packed(messages):
        return [bf16(len(message), BS, BS) for message in messages]

    quarter = bf16(DIAGS, 2, BS // LAYERS, BS)
    shared_quarter = bf16(len(SHARED), 2, BS // LAYERS, BS)
    *pieces, shared = call(
        split_body,
        [quarter] * LAYERS + [bf16(len(SHARED), 2 * LAYERS, BS // LAYERS, BS)],
        2,
        1,
    )(me, presence, blocks)
    shared = swapped(shared)
    pieces = exchanged(pieces)
    own, plus_far, minus_far = call(
        functools.partial(pack_body, DIRECT),
        [bf16(DIAGS, 2, BS, BS)] + packed(DIRECT),
        1,
        LAYERS,
    )(me, *pieces)
    plus_far = from_pair(plus_far, FAR_PAIRS)
    minus_far = from_pair(minus_far, -FAR_PAIRS)
    some = [shared]
    some = call(resplit_body, [shared_quarter] * LAYERS, 1, len(some))(me, *some)
    some = exchanged(some)
    shared, swap_low, swap_high = call(
        shared_body,
        [bf16(len(SHARED), 2, BS, BS)] + packed([SWAP_LOW, SWAP_HIGH]),
        1,
        LAYERS,
    )(me, *some)
    swap_low, swap_high = edge_across(swap_low, -1), edge_across(swap_high, 1)
    before = [own]
    low, high = call(near_body, packed([LOW, HIGH]), 0, len(before))(*before)
    low, high = from_pair(low, -1), from_pair(high, 1)
    before = [shared, swap_low, swap_high, plus_far, minus_far]
    band = call(fan_body, packed([FAN])[0], 0, len(before))(*before)
    plus_band, minus_band = far_across(band, FAR_PAIRS), far_across(band, -FAR_PAIRS)
    arrived = [low, high, plus_far, minus_far]
    edge_low, edge_high = call(
        edge_body, packed([EDGE_LOW, EDGE_HIGH]), 0, len(arrived)
    )(*arrived)
    edge_low, edge_high = from_pair(edge_low, -1), from_pair(edge_high, 1)
    results = call(
        purify_body,
        [quarter] * LAYERS,
        2,
        len(ARRIVE),
        scratch=[
            pltpu.VMEM((WIDTH, WIDTH), jnp.bfloat16),
            pltpu.VMEM((2 * BS, WIDTH), jnp.bfloat16),
            pltpu.VMEM((DIAGS, 2, BS, BS), jnp.bfloat16),
        ],
        flops=4 * 224 * 2 * BS**3,
    )(me, presence, own, *arrived, plus_band, minus_band, edge_low, edge_high)
    results = exchanged(results)
    return call(join_body, bf16(DIAGS, 2 * LAYERS, BS // LAYERS, BS), 1, LAYERS)(
        me, *results
    )


def solution(mesh):
    placed = (P(None, ("row", "col"), "layer", None), P(None, ("row", "col")))
    return jax.shard_map(
        per_device,
        mesh=mesh,
        in_specs=placed,
        out_specs=P(None, ("row", "col"), "layer", None),
        check_vma=False,
    )
```

```python
import functools

import jax
import jax.numpy as jnp
from jax import lax
from jax.experimental import pallas as pl
from jax.experimental.pallas import tpu as pltpu
from jax.sharding import PartitionSpec as P

NBG = 512
BAND = 3
FAR = 160
BS = 128
LAYERS = 4
PAIRS = NBG // 2
FAR_PAIRS = FAR // 2
AXES = ("layer", "row", "col")
OFFSETS = list(range(-BAND, BAND + 1)) + [
    FAR - 1, FAR, FAR + 1, -FAR - 1, -FAR, -FAR + 1,
]
DIAGS = len(OFFSETS)
OFFSET_SET = {value % NBG for value in OFFSETS}

REACH = (
    list(range(-BAND, BAND + 2))
    + list(range(FAR - 1, FAR + 3))
    + list(range(-FAR - 1, -FAR + 3))
)
SLOT = {value % NBG: index for index, value in enumerate(REACH)}
NEAR_END = 8 * BS
PLUS_END = 12 * BS
WIDTH = 16 * BS


def needed(j):
    found = set()
    for i in range(2):
        for left in OFFSETS:
            if (i + left - j) % NBG == 0:
                for b, right in enumerate(OFFSETS):
                    if (left + right) % NBG in OFFSET_SET:
                        found.add(b)
    return sorted(found)


def tiles(rows):
    return [(j, b) for j in rows for b in needed(j)]


BANDS = range(2 * BAND + 1)
ROWS = 2 * LAYERS
SHARED = [1, 2, 3, 4]
PLUS_ROWS = list(range(FAR - 1, FAR + 3))
MINUS_ROWS = list(range(-FAR - 1, -FAR + 3))


def direct_of(rows):
    return sorted({b for j in rows for b in needed(j)} - set(SHARED))


DIRECT = [direct_of(PLUS_ROWS), direct_of(MINUS_ROWS)]
NEAR = [(t, b) for b in range(DIAGS) for t in range(2)] + tiles([-3, -2, -1, 2, 3, 4])
FARS = tiles(PLUS_ROWS) + tiles(MINUS_ROWS)
ARRIVE = [NEAR, FARS]
HALO_LOW = tiles([-3, -2, -1])
HALO_HIGH = [(j + ROWS - 2, b) for j, b in tiles([2, 3, 4])]
EDGE_LOW = [(w, b) for w, j in enumerate((FAR - 1, -FAR - 1)) for b in needed(j)]
EDGE_HIGH = [(w, b) for w, j in enumerate((FAR + 2, -FAR + 2)) for b in needed(j)]


def place_of(p):
    return p % LAYERS * (PAIRS // LAYERS) + p // LAYERS


def moved(x, source_of):
    route = [(place_of(source_of(p)), place_of(p)) for p in range(PAIRS)]
    return lax.ppermute(x, AXES, route)


def across(p):
    cols = LAYERS * 8
    return p - p % cols + (p + cols // 2) % cols


def from_pair(x, distance):
    return moved(x, lambda p: (p + distance) % PAIRS)


def from_group(x, distance):
    return from_pair(x, LAYERS * distance)


def same_group(p, distance):
    return p - p % LAYERS + (p + distance) % LAYERS


def from_layer(x, distance):
    return moved(x, lambda p: same_group(p, distance))


def swapped(x):
    return moved(x, across)


def far_across(x, distance):
    return moved(x, lambda p: across((p + distance) % PAIRS))


def bf16(*shape):
    return jax.ShapeDtypeStruct(shape, jnp.bfloat16)


def call(body, out_shape, n_smem, n_vmem, scratch=(), flops=0, traffic=1 << 22):
    in_specs = [pl.BlockSpec(memory_space=pltpu.SMEM)] * n_smem
    in_specs += [pl.BlockSpec(memory_space=pltpu.VMEM)] * n_vmem
    return pl.pallas_call(
        body,
        out_shape=out_shape,
        in_specs=in_specs,
        out_specs=jax.tree.map(
            lambda _: pl.BlockSpec(memory_space=pltpu.VMEM), out_shape
        ),
        scratch_shapes=list(scratch),
        compiler_params=pltpu.CompilerParams(vmem_limit_bytes=48 << 20),
        cost_estimate=pl.CostEstimate(
            flops=flops, bytes_accessed=traffic, transcendentals=0
        ),
    )


def mask_body(presence_ref, blocks_ref, *out_refs):
    masked_ref, low_ref, high_ref, shared_ref, plus_ref, minus_ref = out_refs
    for row in range(ROWS):
        for d in range(DIAGS):
            tile = blocks_ref[d, row]
            tile = jnp.where(presence_ref[d, row] != 0, tile, jnp.zeros_like(tile))
            masked_ref[d, row] = tile
            if (row - ROWS, d) in HALO_LOW:
                low_ref[HALO_LOW.index((row - ROWS, d))] = tile
            if (row + ROWS, d) in HALO_HIGH:
                high_ref[HALO_HIGH.index((row + ROWS, d))] = tile
            if d in SHARED:
                shared_ref[SHARED.index(d), row] = tile
            for held, ref in zip(DIRECT, (plus_ref, minus_ref)):
                if d in held:
                    ref[held.index(d), row] = tile


def window_pieces(me, message, padded_ref, out_refs, lookup):
    for s, out_ref in enumerate(out_refs):
        start = 2 * lax.rem(me - s + LAYERS, LAYERS)
        for k, tile in enumerate(message):
            slot, row = lookup(tile)
            out_ref[k] = padded_ref[slot, start + row]


def near_body(masked_ref, low_ref, high_ref, *refs):
    out_ref, padded_ref = refs
    padded_ref[:, BAND : BAND + ROWS] = masked_ref[...]
    for message, ref in ((HALO_LOW, low_ref), (HALO_HIGH, high_ref)):
        for k, (row, b) in enumerate(message):
            padded_ref[b, row + BAND] = ref[k]
    for layer in range(LAYERS):
        for k, (j, b) in enumerate(NEAR):
            out_ref[layer, k] = padded_ref[b, 2 * layer + j + BAND]


def held_in(which, b, shared_refs, direct_refs):
    if b in SHARED:
        return shared_refs[which], SHARED.index(b)
    return direct_refs[which], DIRECT[which].index(b)


def edge_body(*refs):
    shared_refs, direct_refs = refs[0:2], refs[2:4]
    for message, row, out_ref in zip((EDGE_LOW, EDGE_HIGH), (ROWS - 1, 0), refs[4:]):
        for k, (which, b) in enumerate(message):
            ref, slot = held_in(which, b, shared_refs, direct_refs)
            out_ref[k] = ref[slot, row]


def fars_body(me_ref, *refs):
    shared_refs, direct_refs, edge_refs = refs[0:2], refs[2:4], refs[4:6]
    out_refs, padded_ref = refs[6 : 6 + LAYERS], refs[6 + LAYERS]
    for which in range(2):
        first = which * DIAGS
        for b in SHARED + DIRECT[which]:
            ref, slot = held_in(which, b, shared_refs, direct_refs)
            padded_ref[first + b, 1 : 1 + ROWS] = ref[slot]
    for message, row, ref in zip((EDGE_LOW, EDGE_HIGH), (0, ROWS + 1), edge_refs):
        for k, (which, b) in enumerate(message):
            padded_ref[which * DIAGS + b, row] = ref[k]

    def lookup(tile):
        j, b = tile
        which = 0 if j > 0 else 1
        return which * DIAGS + b, j - (FAR - 1 if which == 0 else -FAR - 1)

    window_pieces(me_ref[0], FARS, padded_ref, out_refs, lookup)


def placements():
    found = {}
    for operand, message in enumerate(ARRIVE):
        for k, (j, b) in enumerate(message):
            column = SLOT.get((j + OFFSETS[b]) % NBG)
            if column is not None:
                found[SLOT[j % NBG], column] = (operand, k)
    return found


def purify_body(me_ref, presence_ref, *refs):
    fars, outs = refs[1 : 1 + LAYERS], refs[1 + LAYERS : 1 + 2 * LAYERS]
    right_ref, left_ref, result_ref = refs[1 + 2 * LAYERS :]
    sources = ([refs[0].at[layer] for layer in range(LAYERS)], fars)
    me = me_ref[0]
    placed = placements()
    zero = jnp.zeros((BS, BS), jnp.bfloat16)
    starts = [
        [s * (BS // LAYERS) for s in range(LAYERS)],
        [lax.rem(me + s, LAYERS) * (BS // LAYERS) for s in range(LAYERS)],
    ]

    def gather(out_ref, row, column, operand, k):
        for s, piece in enumerate(sources[operand]):
            start = pl.multiple_of(row * BS + starts[operand][s], BS // LAYERS)
            out_ref[pl.ds(start, BS // LAYERS), pl.ds(column * BS, BS)] = piece[k]

    for row in range(16):
        for column in range(16):
            if (row, column) in placed:
                operand, k = placed[row, column]
                gather(right_ref, row, column, operand, k)
            else:
                right_ref[pl.ds(row * BS, BS), pl.ds(column * BS, BS)] = zero
    targets = {
        (i, SLOT[(i + offset) % NBG]): d
        for i in range(2)
        for d, offset in enumerate(OFFSETS)
    }
    for i in range(2):
        for column in range(16):
            d = targets.get((i, column))
            if d is None:
                left_ref[pl.ds(i * BS, BS), pl.ds(column * BS, BS)] = zero
            else:
                gather(left_ref, i, column, 0, NEAR.index((i, d)))

    def dot(left, right):
        return jnp.dot(left, right, preferred_element_type=jnp.float32)

    def product(columns):
        start = columns[0] * BS
        wide = pl.ds(start, len(columns) * BS)
        if start < NEAR_END:
            return dot(left_ref[...], right_ref[:, wide])
        if start < PLUS_END:
            return dot(left_ref[:, :PLUS_END], right_ref[:PLUS_END, wide])
        return dot(left_ref[:, :NEAR_END], right_ref[:NEAR_END, wide]) + dot(
            left_ref[:, PLUS_END:], right_ref[PLUS_END:, wide]
        )

    def each(columns, total, use):
        for at, column in enumerate(columns):
            for i in range(2):
                d = targets.get((i, column))
                if d is not None:
                    tile = total[i * BS : (i + 1) * BS, at * BS : (at + 1) * BS]
                    use(i, column, d, presence_ref[d, 2 * me + i] != 0, tile)

    groups = [[c, c + 1] for c in range(0, 16, 2)]

    def keep_second(i, column, d, present, tile):
        second = jnp.where(present, tile, jnp.zeros_like(tile)).astype(jnp.bfloat16)
        result_ref[d, i] = second

    for columns in groups:
        each(columns, product(columns), keep_second)
    for (i, column), d in targets.items():
        left_ref[pl.ds(i * BS, BS), pl.ds(column * BS, BS)] = result_ref[d, i]

    def keep_result(i, column, d, present, tile):
        third = jnp.where(present, tile, jnp.zeros_like(tile))
        second = result_ref[d, i].astype(jnp.float32)
        result_ref[d, i] = (3.0 * second - 2.0 * third).astype(jnp.bfloat16)

    for columns in groups:
        each(columns, product(columns), keep_result)
    for s, out_ref in enumerate(outs):
        other = lax.rem(me - s + LAYERS, LAYERS)
        start = pl.multiple_of(other * (BS // LAYERS), BS // LAYERS)
        out_ref[...] = result_ref[:, :, pl.ds(start, BS // LAYERS), :]


def join_body(me_ref, *refs):
    me = me_ref[0]
    out_ref = refs[LAYERS]
    for s in range(LAYERS):
        row = 2 * lax.rem(me + s, LAYERS)
        for t in range(2):
            for d in range(DIAGS):
                out_ref[d, row + t] = refs[s][d, t]


def exchanged(pieces):
    far = from_layer(pieces[2], 2)
    return [pieces[0], from_layer(pieces[1], 1), far, from_layer(pieces[3], 3)]


def per_device(blocks, presence):
    me = lax.axis_index("layer").astype(jnp.int32).reshape(1)

    quarters = [
        bf16(DIAGS, ROWS, BS // LAYERS, BS),
        bf16(len(HALO_LOW), BS // LAYERS, BS),
        bf16(len(HALO_HIGH), BS // LAYERS, BS),
    ] + [bf16(len(held), ROWS, BS // LAYERS, BS) for held in [SHARED] + DIRECT]
    masked, low, high, shared, plus, minus = call(mask_body, quarters, 1, 1)(
        presence, blocks
    )
    low, high = from_group(low, -1), from_group(high, 1)
    shared = swapped(shared)
    plus, minus = from_pair(plus, FAR_PAIRS), from_pair(minus, -FAR_PAIRS)
    near = call(
        near_body,
        bf16(LAYERS, len(NEAR), BS // LAYERS, BS),
        0,
        3,
        scratch=[pltpu.VMEM((DIAGS, ROWS + 2 * BAND, BS // LAYERS, BS), jnp.bfloat16)],
    )(masked, low, high)
    near = lax.all_to_all(near, "layer", 0, 0)
    fars = [far_across(shared, FAR_PAIRS), far_across(shared, -FAR_PAIRS), plus, minus]
    edges = call(
        edge_body,
        [bf16(len(m), BS // LAYERS, BS) for m in (EDGE_LOW, EDGE_HIGH)],
        0,
        4,
    )(*fars)
    edges = [from_group(edges[0], -1), from_group(edges[1], 1)]
    fars = call(
        fars_body,
        [bf16(len(FARS), BS // LAYERS, BS)] * LAYERS,
        1,
        6,
        scratch=[pltpu.VMEM((2 * DIAGS, ROWS + 2, BS // LAYERS, BS), jnp.bfloat16)],
    )(me, *fars, *edges)
    fars = exchanged(fars)
    results = call(
        purify_body,
        [bf16(DIAGS, 2, BS // LAYERS, BS)] * LAYERS,
        2,
        1 + LAYERS,
        scratch=[
            pltpu.VMEM((WIDTH, WIDTH), jnp.bfloat16),
            pltpu.VMEM((2 * BS, WIDTH), jnp.bfloat16),
            pltpu.VMEM((DIAGS, 2, BS, BS), jnp.bfloat16),
        ],
        flops=4 * 224 * 2 * BS**3,
    )(me, presence, near, *fars)
    results = exchanged(results)
    return call(join_body, bf16(DIAGS, 2 * LAYERS, BS // LAYERS, BS), 1, LAYERS)(
        me, *results
    )


def solution(mesh):
    placed = (P(None, ("row", "col"), "layer", None), P(None, ("row", "col")))
    return jax.shard_map(
        per_device,
        mesh=mesh,
        in_specs=placed,
        out_specs=P(None, ("row", "col"), "layer", None),
        check_vma=False,
    )
```

```python
import functools

import jax
import jax.numpy as jnp
from jax import lax
from jax.experimental import pallas as pl
from jax.experimental.pallas import tpu as pltpu
from jax.sharding import PartitionSpec as P

NBG = 512
BAND = 3
FAR = 160
BS = 128
LAYERS = 4
PAIRS = NBG // 2
FAR_PAIRS = FAR // 2
AXES = ("layer", "row", "col")
OFFSETS = list(range(-BAND, BAND + 1)) + [
    FAR - 1, FAR, FAR + 1, -FAR - 1, -FAR, -FAR + 1,
]
DIAGS = len(OFFSETS)
OFFSET_SET = {value % NBG for value in OFFSETS}

REACH = (
    list(range(-BAND, BAND + 2))
    + list(range(FAR - 1, FAR + 3))
    + list(range(-FAR - 1, -FAR + 3))
)
SLOT = {value % NBG: index for index, value in enumerate(REACH)}
NEAR_END = 8 * BS
PLUS_END = 12 * BS
WIDTH = 16 * BS


def needed(j):
    found = set()
    for i in range(2):
        for left in OFFSETS:
            if (i + left - j) % NBG == 0:
                for b, right in enumerate(OFFSETS):
                    if (left + right) % NBG in OFFSET_SET:
                        found.add(b)
    return sorted(found)


BANDS = range(2 * BAND + 1)
SHARED = sorted(b for b in set().union(*(needed(FAR + t) for t in range(-1, 3))) if b in BANDS)


def band_of(j):
    return [b for b in needed(j) if b in BANDS]


def far_of(j):
    return [b for b in needed(j) if b not in BANDS]


def tiles(rows, which=needed):
    return [(j, b) for j in rows for b in which(j)]


OWN = [(t, b) for b in range(DIAGS) for t in range(2)]
LOW, HIGH = tiles([-2, -1]), tiles([2, 3])
FAN = tiles(range(FAR - 1, FAR + 3), band_of)
PLUS_BAND = FAN
MINUS_BAND = [(j - 2 * FAR, b) for j, b in FAN]
PLUS_FAR = tiles([FAR, FAR + 1], far_of)
MINUS_FAR = tiles([-FAR, -FAR + 1], far_of)
EDGE_LOW = tiles([-3]) + tiles([FAR - 1, -FAR - 1], far_of)
EDGE_HIGH = tiles([4]) + tiles([FAR + 2, -FAR + 2], far_of)
MAIN = [LOW, HIGH, PLUS_FAR, MINUS_FAR]
ARRIVE = [OWN] + MAIN + [PLUS_BAND, MINUS_BAND, EDGE_LOW, EDGE_HIGH]
NEAR = [[(j % 2, b) for j, b in message] for message in (LOW, HIGH)]
SWAP_LOW = [(1, b) for b in band_of(FAR - 1)]
SWAP_HIGH = [(0, b) for b in band_of(FAR + 2)]
DIRECT = [[(j % 2, b) for j, b in message] for message in (PLUS_FAR, MINUS_FAR)]


def place_of(p):
    return p % LAYERS * (PAIRS // LAYERS) + p // LAYERS


def moved(x, source_of):
    route = [(place_of(source_of(p)), place_of(p)) for p in range(PAIRS)]
    return lax.ppermute(x, AXES, route)


def across(p):
    cols = LAYERS * 8
    return p - p % cols + (p + cols // 2) % cols


def from_pair(x, distance):
    return moved(x, lambda p: (p + distance) % PAIRS)


def same_group(p, distance):
    return p - p % LAYERS + (p + distance) % LAYERS


def from_layer(x, distance):
    return moved(x, lambda p: same_group(p, distance))


def swapped(x):
    return moved(x, across)


def edge_across(x, distance):
    return moved(x, lambda p: across((across(p) + distance) % PAIRS))


def far_across(x, distance):
    return moved(x, lambda p: across((p + distance) % PAIRS))


def bf16(*shape):
    return jax.ShapeDtypeStruct(shape, jnp.bfloat16)


def call(body, out_shape, n_smem, n_vmem, scratch=(), flops=0, traffic=1 << 22):
    in_specs = [pl.BlockSpec(memory_space=pltpu.SMEM)] * n_smem
    in_specs += [pl.BlockSpec(memory_space=pltpu.VMEM)] * n_vmem
    return pl.pallas_call(
        body,
        out_shape=out_shape,
        in_specs=in_specs,
        out_specs=jax.tree.map(
            lambda _: pl.BlockSpec(memory_space=pltpu.VMEM), out_shape
        ),
        scratch_shapes=list(scratch),
        compiler_params=pltpu.CompilerParams(vmem_limit_bytes=48 << 20),
        cost_estimate=pl.CostEstimate(
            flops=flops, bytes_accessed=traffic, transcendentals=0
        ),
    )


def split_body(me_ref, presence_ref, blocks_ref, *out_refs):
    me = me_ref[0]
    shared_ref = out_refs[LAYERS]
    for s in range(LAYERS):
        other = lax.rem(me - s + LAYERS, LAYERS)
        for t in range(2):
            row = 2 * other + t
            for d in range(DIAGS):
                tile = blocks_ref[d, row]
                present = presence_ref[d, row] != 0
                tile = jnp.where(present, tile, jnp.zeros_like(tile))
                out_refs[s][d, t] = tile
                if d in SHARED:
                    shared_ref[SHARED.index(d), row] = tile


def resplit_body(shared_ref, *refs):
    out_ref = refs[-1]
    for layer in range(LAYERS):
        for t in range(2):
            for k in range(len(SHARED)):
                out_ref[layer, k, t] = shared_ref[k, 2 * layer + t]


def gather_pieces(me, pieces, out_ref):
    for s, piece in enumerate(pieces):
        other = lax.rem(me + s, LAYERS)
        start = pl.multiple_of(other * (BS // LAYERS), BS // LAYERS)
        out_ref[:, :, pl.ds(start, BS // LAYERS), :] = piece[...]


def pack_body(messages, me_ref, *refs):
    pieces, own_ref, out_refs = refs[:LAYERS], refs[LAYERS], refs[LAYERS + 1 :]
    gather_pieces(me_ref[0], pieces, own_ref)
    for message, out_ref in zip(messages, out_refs):
        for k, (t, b) in enumerate(message):
            out_ref[k] = own_ref[b, t]


def near_body(own_ref, *refs):
    for message, out_ref in zip(NEAR, refs[-2:]):
        for k, (t, b) in enumerate(message):
            out_ref[k] = own_ref[b, t]


def shared_body(pieces_ref, shared_ref, *out_refs):
    for layer in range(LAYERS):
        rows = pl.ds(layer * (BS // LAYERS), BS // LAYERS)
        shared_ref[:, :, rows, :] = pieces_ref[layer]
    for message, out_ref in zip((SWAP_LOW, SWAP_HIGH), out_refs):
        for k, (t, b) in enumerate(message):
            out_ref[k] = shared_ref[SHARED.index(b), t]


def fan_body(shared_ref, low_ref, high_ref, *refs):
    out_ref = refs[-1]
    for k, (j, b) in enumerate(FAN):
        t = j - FAR
        if t < 0:
            out_ref[k] = low_ref[SWAP_LOW.index((1, b))]
        elif t > 1:
            out_ref[k] = high_ref[SWAP_HIGH.index((0, b))]
        else:
            out_ref[k] = shared_ref[SHARED.index(b), t]


def edge_body(*refs):
    sources, out_refs = refs[: len(MAIN)], refs[len(MAIN) :]
    for shift, message, out_ref in zip((2, -2), (EDGE_LOW, EDGE_HIGH), out_refs):
        for k, (j, b) in enumerate(message):
            [(ref, held)] = [
                (ref, held)
                for ref, held in zip(sources, MAIN)
                if (j + shift, b) in held
            ]
            out_ref[k] = ref[held.index((j + shift, b))]


def placements():
    found = {}
    for operand, message in enumerate(ARRIVE):
        for k, (j, b) in enumerate(message):
            column = SLOT.get((j + OFFSETS[b]) % NBG)
            if column is not None:
                found[SLOT[j % NBG], column] = (operand, k if operand else (b, j))
    return found


def purify_body(me_ref, presence_ref, *refs):
    sources, outs = refs[: len(ARRIVE)], refs[len(ARRIVE) : len(ARRIVE) + LAYERS]
    right_ref, left_ref, result_ref = refs[len(ARRIVE) + LAYERS :]
    me = me_ref[0]
    placed = placements()
    zero = jnp.zeros((BS, BS), jnp.bfloat16)
    for row in range(16):
        for column in range(16):
            where = (pl.ds(row * BS, BS), pl.ds(column * BS, BS))
            if (row, column) in placed:
                operand, index = placed[row, column]
                right_ref[where] = sources[operand][index]
            else:
                right_ref[where] = zero
    targets = {
        (i, SLOT[(i + offset) % NBG]): d
        for i in range(2)
        for d, offset in enumerate(OFFSETS)
    }
    for i in range(2):
        for column in range(16):
            where = (pl.ds(i * BS, BS), pl.ds(column * BS, BS))
            d = targets.get((i, column))
            left_ref[where] = zero if d is None else sources[0][d, i]

    def dot(left, right):
        return jnp.dot(left, right, preferred_element_type=jnp.float32)

    def product(columns):
        start = columns[0] * BS
        wide = pl.ds(start, len(columns) * BS)
        if start < NEAR_END:
            return dot(left_ref[...], right_ref[:, wide])
        if start < PLUS_END:
            return dot(left_ref[:, :PLUS_END], right_ref[:PLUS_END, wide])
        return dot(left_ref[:, :NEAR_END], right_ref[:NEAR_END, wide]) + dot(
            left_ref[:, PLUS_END:], right_ref[PLUS_END:, wide]
        )

    def each(columns, total, use):
        for at, column in enumerate(columns):
            for i in range(2):
                d = targets.get((i, column))
                if d is not None:
                    tile = total[i * BS : (i + 1) * BS, at * BS : (at + 1) * BS]
                    use(i, column, d, presence_ref[d, 2 * me + i] != 0, tile)

    groups = [[c, c + 1] for c in range(0, 16, 2)]

    def keep_second(i, column, d, present, tile):
        second = jnp.where(present, tile, jnp.zeros_like(tile)).astype(jnp.bfloat16)
        result_ref[d, i] = second

    for columns in groups:
        each(columns, product(columns), keep_second)
    for (i, column), d in targets.items():
        left_ref[pl.ds(i * BS, BS), pl.ds(column * BS, BS)] = result_ref[d, i]

    def keep_result(i, column, d, present, tile):
        third = jnp.where(present, tile, jnp.zeros_like(tile))
        second = result_ref[d, i].astype(jnp.float32)
        result_ref[d, i] = (3.0 * second - 2.0 * third).astype(jnp.bfloat16)

    for columns in groups:
        each(columns, product(columns), keep_result)
    for s, out_ref in enumerate(outs):
        other = lax.rem(me - s + LAYERS, LAYERS)
        start = pl.multiple_of(other * (BS // LAYERS), BS // LAYERS)
        out_ref[...] = result_ref[:, :, pl.ds(start, BS // LAYERS), :]


def join_body(me_ref, *refs):
    me = me_ref[0]
    out_ref = refs[LAYERS]
    for s in range(LAYERS):
        row = 2 * lax.rem(me + s, LAYERS)
        for t in range(2):
            for d in range(DIAGS):
                out_ref[d, row + t] = refs[s][d, t]


def exchanged(pieces):
    far = from_layer(pieces[2], 2)
    return [pieces[0], from_layer(pieces[1], 1), far, from_layer(pieces[3], 3)]


def per_device(blocks, presence):
    me = lax.axis_index("layer").astype(jnp.int32).reshape(1)

    def packed(messages):
        return [bf16(len(message), BS, BS) for message in messages]

    quarter = bf16(DIAGS, 2, BS // LAYERS, BS)
    *pieces, shared = call(
        split_body,
        [quarter] * LAYERS + [bf16(len(SHARED), 2 * LAYERS, BS // LAYERS, BS)],
        2,
        1,
    )(me, presence, blocks)
    shared = swapped(shared)
    pieces = exchanged(pieces)
    own, plus_far, minus_far = call(
        functools.partial(pack_body, DIRECT),
        [bf16(DIAGS, 2, BS, BS)] + packed(DIRECT),
        1,
        LAYERS,
    )(me, *pieces)
    plus_far = from_pair(plus_far, FAR_PAIRS)
    minus_far = from_pair(minus_far, -FAR_PAIRS)
    some = [shared]
    some = call(
        resplit_body, bf16(LAYERS, len(SHARED), 2, BS // LAYERS, BS), 0, len(some)
    )(*some)
    piece = some
    some = lax.all_to_all(some, "layer", 0, 0)
    shared, swap_low, swap_high = call(
        shared_body,
        [bf16(len(SHARED), 2, BS, BS)] + packed([SWAP_LOW, SWAP_HIGH]),
        0,
        1,
    )(some)
    swap_low, swap_high = edge_across(swap_low, -1), edge_across(swap_high, 1)
    before = [own, piece]
    low, high = call(near_body, packed([LOW, HIGH]), 0, len(before))(*before)
    low, high = from_pair(low, -1), from_pair(high, 1)
    before = [shared, swap_low, swap_high, plus_far, minus_far]
    band = call(fan_body, packed([FAN])[0], 0, len(before))(*before)
    plus_band, minus_band = far_across(band, FAR_PAIRS), far_across(band, -FAR_PAIRS)
    arrived = [low, high, plus_far, minus_far]
    edge_low, edge_high = call(
        edge_body, packed([EDGE_LOW, EDGE_HIGH]), 0, len(arrived)
    )(*arrived)
    edge_low, edge_high = from_pair(edge_low, -1), from_pair(edge_high, 1)
    results = call(
        purify_body,
        [quarter] * LAYERS,
        2,
        len(ARRIVE),
        scratch=[
            pltpu.VMEM((WIDTH, WIDTH), jnp.bfloat16),
            pltpu.VMEM((2 * BS, WIDTH), jnp.bfloat16),
            pltpu.VMEM((DIAGS, 2, BS, BS), jnp.bfloat16),
        ],
        flops=4 * 224 * 2 * BS**3,
    )(me, presence, own, *arrived, plus_band, minus_band, edge_low, edge_high)
    results = exchanged(results)
    return call(join_body, bf16(DIAGS, 2 * LAYERS, BS // LAYERS, BS), 1, LAYERS)(
        me, *results
    )


def solution(mesh):
    placed = (P(None, ("row", "col"), "layer", None), P(None, ("row", "col")))
    return jax.shard_map(
        per_device,
        mesh=mesh,
        in_specs=placed,
        out_specs=P(None, ("row", "col"), "layer", None),
        check_vma=False,
    )
```

```python
import functools

import jax
import jax.numpy as jnp
from jax import lax
from jax.experimental import pallas as pl
from jax.experimental.pallas import tpu as pltpu
from jax.sharding import PartitionSpec as P

NBG = 512
BAND = 3
FAR = 160
BS = 128
LAYERS = 4
PAIRS = NBG // 2
FAR_PAIRS = FAR // 2
AXES = ("layer", "row", "col")
OFFSETS = list(range(-BAND, BAND + 1)) + [
    FAR - 1, FAR, FAR + 1, -FAR - 1, -FAR, -FAR + 1,
]
DIAGS = len(OFFSETS)
OFFSET_SET = {value % NBG for value in OFFSETS}

REACH = (
    list(range(-BAND, BAND + 2))
    + list(range(FAR - 1, FAR + 3))
    + list(range(-FAR - 1, -FAR + 3))
)
SLOT = {value % NBG: index for index, value in enumerate(REACH)}
NEAR_END = 8 * BS
PLUS_END = 12 * BS
WIDTH = 16 * BS


def needed(j):
    found = set()
    for i in range(2):
        for left in OFFSETS:
            if (i + left - j) % NBG == 0:
                for b, right in enumerate(OFFSETS):
                    if (left + right) % NBG in OFFSET_SET:
                        found.add(b)
    return sorted(found)


BANDS = range(2 * BAND + 1)
SHARED = sorted(b for b in set().union(*(needed(FAR + t) for t in range(-1, 3))) if b in BANDS)


def band_of(j):
    return [b for b in needed(j) if b in BANDS]


def far_of(j):
    return [b for b in needed(j) if b not in BANDS]


def tiles(rows, which=needed):
    return [(j, b) for j in rows for b in which(j)]


OWN = [(t, b) for b in range(DIAGS) for t in range(2)]
LOW, HIGH = tiles([-2, -1]), tiles([2, 3])
LOWER, HIGHER = tiles([-3]), tiles([4])
FAN = [(FAR + t, b) for t in range(2) for b in SHARED]
PLUS_BAND = FAN
MINUS_BAND = [(j - 2 * FAR, b) for j, b in FAN]
PLUS_FAR = tiles([FAR, FAR + 1], far_of)
MINUS_FAR = tiles([-FAR, -FAR + 1], far_of)
EDGE_LOW = tiles([FAR - 1, -FAR - 1])
EDGE_HIGH = tiles([FAR + 2, -FAR + 2])
MAIN = [PLUS_FAR, MINUS_FAR, PLUS_BAND, MINUS_BAND]
ARRIVE = [OWN, LOW, HIGH, LOWER, HIGHER] + MAIN + [EDGE_LOW, EDGE_HIGH]
NEAR = [[(j % 2, b) for j, b in message] for message in (LOW, HIGH, LOWER, HIGHER)]
DIRECT = [[(j % 2, b) for j, b in message] for message in (PLUS_FAR, MINUS_FAR)]


def place_of(p):
    return p % LAYERS * (PAIRS // LAYERS) + p // LAYERS


def moved(x, source_of):
    route = [(place_of(source_of(p)), place_of(p)) for p in range(PAIRS)]
    return lax.ppermute(x, AXES, route)


def across(p):
    cols = LAYERS * 8
    return p - p % cols + (p + cols // 2) % cols


def from_pair(x, distance):
    return moved(x, lambda p: (p + distance) % PAIRS)


def same_group(p, distance):
    return p - p % LAYERS + (p + distance) % LAYERS


def from_layer(x, distance):
    return moved(x, lambda p: same_group(p, distance))


def swapped(x):
    return moved(x, across)


def far_across(x, distance):
    return moved(x, lambda p: across((p + distance) % PAIRS))


def bf16(*shape):
    return jax.ShapeDtypeStruct(shape, jnp.bfloat16)


def call(body, out_shape, n_smem, n_vmem, scratch=(), flops=0, traffic=1 << 22):
    in_specs = [pl.BlockSpec(memory_space=pltpu.SMEM)] * n_smem
    in_specs += [pl.BlockSpec(memory_space=pltpu.VMEM)] * n_vmem
    return pl.pallas_call(
        body,
        out_shape=out_shape,
        in_specs=in_specs,
        out_specs=jax.tree.map(
            lambda _: pl.BlockSpec(memory_space=pltpu.VMEM), out_shape
        ),
        scratch_shapes=list(scratch),
        compiler_params=pltpu.CompilerParams(vmem_limit_bytes=48 << 20),
        cost_estimate=pl.CostEstimate(
            flops=flops, bytes_accessed=traffic, transcendentals=0
        ),
    )


def split_body(me_ref, presence_ref, blocks_ref, *out_refs):
    me = me_ref[0]
    shared_ref = out_refs[LAYERS]
    for s in range(LAYERS):
        other = lax.rem(me - s + LAYERS, LAYERS)
        for t in range(2):
            row = 2 * other + t
            for d in range(DIAGS):
                tile = blocks_ref[d, row]
                present = presence_ref[d, row] != 0
                tile = jnp.where(present, tile, jnp.zeros_like(tile))
                out_refs[s][d, t] = tile
                if d in SHARED:
                    shared_ref[SHARED.index(d), row] = tile


def resplit_body(me_ref, shared_ref, *out_refs):
    for s, out_ref in enumerate(out_refs[-LAYERS:]):
        row = 2 * lax.rem(me_ref[0] - s + LAYERS, LAYERS)
        for t in range(2):
            for k in range(len(SHARED)):
                out_ref[k, t] = shared_ref[k, row + t]


def gather_pieces(me, pieces, out_ref):
    for s, piece in enumerate(pieces):
        other = lax.rem(me + s, LAYERS)
        start = pl.multiple_of(other * (BS // LAYERS), BS // LAYERS)
        out_ref[:, :, pl.ds(start, BS // LAYERS), :] = piece[...]


def pack_body(messages, me_ref, *refs):
    pieces, own_ref, out_refs = refs[:LAYERS], refs[LAYERS], refs[LAYERS + 1 :]
    gather_pieces(me_ref[0], pieces, own_ref)
    for message, out_ref in zip(messages, out_refs):
        for k, (t, b) in enumerate(message):
            out_ref[k] = own_ref[b, t]


def near_body(own_ref, *refs):
    for message, out_ref in zip(NEAR, refs[-len(NEAR) :]):
        for k, (t, b) in enumerate(message):
            out_ref[k] = own_ref[b, t]


def fan_body(me_ref, *refs):
    pieces, out_ref = refs[:LAYERS], refs[LAYERS]
    for s, piece in enumerate(pieces):
        other = lax.rem(me_ref[0] + s, LAYERS)
        rows = pl.ds(pl.multiple_of(other * (BS // LAYERS), BS // LAYERS), BS // LAYERS)
        for k, (j, b) in enumerate(FAN):
            out_ref[k, rows, :] = piece[SHARED.index(b), j - FAR]


def edge_body(*refs):
    sources, out_refs = refs[: len(MAIN)], refs[len(MAIN) :]
    for shift, message, out_ref in zip((2, -2), (EDGE_LOW, EDGE_HIGH), out_refs):
        for k, (j, b) in enumerate(message):
            [(ref, held)] = [
                (ref, held)
                for ref, held in zip(sources, MAIN)
                if (j + shift, b) in held
            ]
            out_ref[k] = ref[held.index((j + shift, b))]


def placements():
    found = {}
    for operand, message in enumerate(ARRIVE):
        for k, (j, b) in enumerate(message):
            column = SLOT.get((j + OFFSETS[b]) % NBG)
            if column is not None:
                found[SLOT[j % NBG], column] = (operand, k if operand else (b, j))
    return found


def purify_body(me_ref, presence_ref, *refs):
    sources, outs = refs[: len(ARRIVE)], refs[len(ARRIVE) : len(ARRIVE) + LAYERS]
    right_ref, left_ref, result_ref = refs[len(ARRIVE) + LAYERS :]
    me = me_ref[0]
    placed = placements()
    zero = jnp.zeros((BS, BS), jnp.bfloat16)
    for row in range(16):
        for column in range(16):
            where = (pl.ds(row * BS, BS), pl.ds(column * BS, BS))
            if (row, column) in placed:
                operand, index = placed[row, column]
                right_ref[where] = sources[operand][index]
            else:
                right_ref[where] = zero
    targets = {
        (i, SLOT[(i + offset) % NBG]): d
        for i in range(2)
        for d, offset in enumerate(OFFSETS)
    }
    for i in range(2):
        for column in range(16):
            where = (pl.ds(i * BS, BS), pl.ds(column * BS, BS))
            d = targets.get((i, column))
            left_ref[where] = zero if d is None else sources[0][d, i]

    def dot(left, right):
        return jnp.dot(left, right, preferred_element_type=jnp.float32)

    def product(columns):
        start = columns[0] * BS
        wide = pl.ds(start, len(columns) * BS)
        if start < NEAR_END:
            return dot(left_ref[...], right_ref[:, wide])
        if start < PLUS_END:
            return dot(left_ref[:, :PLUS_END], right_ref[:PLUS_END, wide])
        return dot(left_ref[:, :NEAR_END], right_ref[:NEAR_END, wide]) + dot(
            left_ref[:, PLUS_END:], right_ref[PLUS_END:, wide]
        )

    def each(columns, total, use):
        for at, column in enumerate(columns):
            for i in range(2):
                d = targets.get((i, column))
                if d is not None:
                    tile = total[i * BS : (i + 1) * BS, at * BS : (at + 1) * BS]
                    use(i, column, d, presence_ref[d, 2 * me + i] != 0, tile)

    groups = [[c, c + 1] for c in range(0, 16, 2)]

    def keep_second(i, column, d, present, tile):
        second = jnp.where(present, tile, jnp.zeros_like(tile)).astype(jnp.bfloat16)
        result_ref[d, i] = second

    for columns in groups:
        each(columns, product(columns), keep_second)
    for (i, column), d in targets.items():
        left_ref[pl.ds(i * BS, BS), pl.ds(column * BS, BS)] = result_ref[d, i]

    def keep_result(i, column, d, present, tile):
        third = jnp.where(present, tile, jnp.zeros_like(tile))
        second = result_ref[d, i].astype(jnp.float32)
        result_ref[d, i] = (3.0 * second - 2.0 * third).astype(jnp.bfloat16)

    for columns in groups:
        each(columns, product(columns), keep_result)
    for s, out_ref in enumerate(outs):
        other = lax.rem(me - s + LAYERS, LAYERS)
        start = pl.multiple_of(other * (BS // LAYERS), BS // LAYERS)
        out_ref[...] = result_ref[:, :, pl.ds(start, BS // LAYERS), :]


def join_body(me_ref, *refs):
    me = me_ref[0]
    out_ref = refs[LAYERS]
    for s in range(LAYERS):
        row = 2 * lax.rem(me + s, LAYERS)
        for t in range(2):
            for d in range(DIAGS):
                out_ref[d, row + t] = refs[s][d, t]


def exchanged(pieces):
    far = from_layer(pieces[2], 2)
    return [pieces[0], from_layer(pieces[1], 1), far, from_layer(pieces[3], 3)]


def per_device(blocks, presence):
    me = lax.axis_index("layer").astype(jnp.int32).reshape(1)

    def packed(messages):
        return [bf16(len(message), BS, BS) for message in messages]

    quarter = bf16(DIAGS, 2, BS // LAYERS, BS)
    shared_quarter = bf16(len(SHARED), 2, BS // LAYERS, BS)
    *pieces, shared = call(
        split_body,
        [quarter] * LAYERS + [bf16(len(SHARED), 2 * LAYERS, BS // LAYERS, BS)],
        2,
        1,
    )(me, presence, blocks)
    shared = swapped(shared)
    pieces = exchanged(pieces)
    own, plus_far, minus_far = call(
        functools.partial(pack_body, DIRECT),
        [bf16(DIAGS, 2, BS, BS)] + packed(DIRECT),
        1,
        LAYERS,
    )(me, *pieces)
    plus_far = from_pair(plus_far, FAR_PAIRS)
    minus_far = from_pair(minus_far, -FAR_PAIRS)
    some = [shared, own]
    some = call(resplit_body, [shared_quarter] * LAYERS, 1, len(some))(me, *some)
    some = exchanged(some)
    band = call(fan_body, packed([FAN])[0], 1, LAYERS)(me, *some)
    plus_band, minus_band = far_across(band, FAR_PAIRS), far_across(band, -FAR_PAIRS)
    before = [own, band]
    low, high, lower, higher = call(near_body, packed(NEAR), 0, len(before))(*before)
    low, high = from_pair(low, -1), from_pair(high, 1)
    lower, higher = from_pair(lower, -2), from_pair(higher, 2)
    arrived = [plus_far, minus_far, plus_band, minus_band]
    edge_low, edge_high = call(
        edge_body, packed([EDGE_LOW, EDGE_HIGH]), 0, len(arrived)
    )(*arrived)
    edge_low, edge_high = from_pair(edge_low, -1), from_pair(edge_high, 1)
    results = call(
        purify_body,
        [quarter] * LAYERS,
        2,
        len(ARRIVE),
        scratch=[
            pltpu.VMEM((WIDTH, WIDTH), jnp.bfloat16),
            pltpu.VMEM((2 * BS, WIDTH), jnp.bfloat16),
            pltpu.VMEM((DIAGS, 2, BS, BS), jnp.bfloat16),
        ],
        flops=4 * 224 * 2 * BS**3,
    )(me, presence, own, low, high, lower, higher, *arrived, edge_low, edge_high)
    results = exchanged(results)
    return call(join_body, bf16(DIAGS, 2 * LAYERS, BS // LAYERS, BS), 1, LAYERS)(
        me, *results
    )


def solution(mesh):
    placed = (P(None, ("row", "col"), "layer", None), P(None, ("row", "col")))
    return jax.shard_map(
        per_device,
        mesh=mesh,
        in_specs=placed,
        out_specs=P(None, ("row", "col"), "layer", None),
        check_vma=False,
    )
```

```python
import functools

import jax
import jax.numpy as jnp
from jax import lax
from jax.experimental import pallas as pl
from jax.experimental.pallas import tpu as pltpu
from jax.sharding import PartitionSpec as P

NBG = 512
BAND = 3
FAR = 160
BS = 128
LAYERS = 4
PAIRS = NBG // 2
FAR_PAIRS = FAR // 2
AXES = ("layer", "row", "col")
OFFSETS = list(range(-BAND, BAND + 1)) + [
    FAR - 1, FAR, FAR + 1, -FAR - 1, -FAR, -FAR + 1,
]
DIAGS = len(OFFSETS)
OFFSET_SET = {value % NBG for value in OFFSETS}

REACH = (
    list(range(-BAND, BAND + 2))
    + list(range(FAR - 1, FAR + 3))
    + list(range(-FAR - 1, -FAR + 3))
)
SLOT = {value % NBG: index for index, value in enumerate(REACH)}
NEAR_END = 8 * BS
PLUS_END = 12 * BS
WIDTH = 16 * BS


def needed(j):
    found = set()
    for i in range(2):
        for left in OFFSETS:
            if (i + left - j) % NBG == 0:
                for b, right in enumerate(OFFSETS):
                    if (left + right) % NBG in OFFSET_SET:
                        found.add(b)
    return sorted(found)


BANDS = range(2 * BAND + 1)
SHARED = sorted(b for b in set().union(*(needed(FAR + t) for t in range(-1, 3))) if b in BANDS)


def band_of(j):
    return [b for b in needed(j) if b in BANDS]


def far_of(j):
    return [b for b in needed(j) if b not in BANDS]


def tiles(rows, which=needed):
    return [(j, b) for j in rows for b in which(j)]


OWN = [(t, b) for b in range(DIAGS) for t in range(2)]
LOW, HIGH = tiles([-2, -1]), tiles([2, 3])
LOWER, HIGHER = tiles([-3]), tiles([4])
FAN = [(FAR + t, b) for t in range(2) for b in SHARED]
PLUS_BAND = FAN
MINUS_BAND = [(j - 2 * FAR, b) for j, b in FAN]
PLUS_FAR = tiles([FAR, FAR + 1], far_of)
MINUS_FAR = tiles([-FAR, -FAR + 1], far_of)
EDGE_LOW = tiles([FAR - 1, -FAR - 1])
EDGE_HIGH = tiles([FAR + 2, -FAR + 2])
MAIN = [PLUS_FAR, MINUS_FAR, PLUS_BAND, MINUS_BAND]
ARRIVE = [OWN, LOW, HIGH, LOWER, HIGHER] + MAIN + [EDGE_LOW, EDGE_HIGH]
NEAR = [[(j % 2, b) for j, b in message] for message in (LOW, HIGH, LOWER, HIGHER)]
DIRECT = [[(j % 2, b) for j, b in message] for message in (PLUS_FAR, MINUS_FAR)]


def place_of(p):
    return p % LAYERS * (PAIRS // LAYERS) + p // LAYERS


def moved(x, source_of):
    route = [(place_of(source_of(p)), place_of(p)) for p in range(PAIRS)]
    return lax.ppermute(x, AXES, route)


def across(p):
    cols = LAYERS * 8
    return p - p % cols + (p + cols // 2) % cols


def from_pair(x, distance):
    return moved(x, lambda p: (p + distance) % PAIRS)


def same_group(p, distance):
    return p - p % LAYERS + (p + distance) % LAYERS


def from_layer(x, distance):
    return moved(x, lambda p: same_group(p, distance))


def swapped(x):
    return moved(x, across)


def far_across(x, distance):
    return moved(x, lambda p: across((p + distance) % PAIRS))


def bf16(*shape):
    return jax.ShapeDtypeStruct(shape, jnp.bfloat16)


def call(body, out_shape, n_smem, n_vmem, scratch=(), flops=0, traffic=1 << 22):
    in_specs = [pl.BlockSpec(memory_space=pltpu.SMEM)] * n_smem
    in_specs += [pl.BlockSpec(memory_space=pltpu.VMEM)] * n_vmem
    return pl.pallas_call(
        body,
        out_shape=out_shape,
        in_specs=in_specs,
        out_specs=jax.tree.map(
            lambda _: pl.BlockSpec(memory_space=pltpu.VMEM), out_shape
        ),
        scratch_shapes=list(scratch),
        compiler_params=pltpu.CompilerParams(vmem_limit_bytes=48 << 20),
        cost_estimate=pl.CostEstimate(
            flops=flops, bytes_accessed=traffic, transcendentals=0
        ),
    )


def split_body(me_ref, presence_ref, blocks_ref, *out_refs):
    me = me_ref[0]
    shared_ref = out_refs[LAYERS]
    for s in range(LAYERS):
        other = lax.rem(me - s + LAYERS, LAYERS)
        for t in range(2):
            row = 2 * other + t
            for d in range(DIAGS):
                tile = blocks_ref[d, row]
                present = presence_ref[d, row] != 0
                tile = jnp.where(present, tile, jnp.zeros_like(tile))
                out_refs[s][d, t] = tile
                if d in SHARED:
                    shared_ref[SHARED.index(d), row] = tile


def resplit_body(me_ref, shared_ref, *out_refs):
    for s, out_ref in enumerate(out_refs[-LAYERS:]):
        row = 2 * lax.rem(me_ref[0] - s + LAYERS, LAYERS)
        for t in range(2):
            for k in range(len(SHARED)):
                out_ref[k, t] = shared_ref[k, row + t]


def gather_pieces(me, pieces, out_ref):
    for s, piece in enumerate(pieces):
        other = lax.rem(me + s, LAYERS)
        start = pl.multiple_of(other * (BS // LAYERS), BS // LAYERS)
        out_ref[:, :, pl.ds(start, BS // LAYERS), :] = piece[...]


def pack_body(messages, me_ref, *refs):
    pieces, own_ref, out_refs = refs[:LAYERS], refs[LAYERS], refs[LAYERS + 1 :]
    gather_pieces(me_ref[0], pieces, own_ref)
    for message, out_ref in zip(messages, out_refs):
        for k, (t, b) in enumerate(message):
            out_ref[k] = own_ref[b, t]


def near_body(own_ref, *refs):
    for message, out_ref in zip(NEAR[:2], refs[-2:]):
        for k, (t, b) in enumerate(message):
            out_ref[k] = own_ref[b, t]


def fan_body(me_ref, *refs):
    pieces, out_ref = refs[:LAYERS], refs[LAYERS]
    for s, piece in enumerate(pieces):
        other = lax.rem(me_ref[0] + s, LAYERS)
        rows = pl.ds(pl.multiple_of(other * (BS // LAYERS), BS // LAYERS), BS // LAYERS)
        for k, (j, b) in enumerate(FAN):
            out_ref[k, rows, :] = piece[SHARED.index(b), j - FAR]


def edge_body(*refs):
    sources, out_refs = refs[: len(MAIN)], refs[len(MAIN) :]
    for shift, message, out_ref in zip((2, -2), (EDGE_LOW, EDGE_HIGH), out_refs):
        for k, (j, b) in enumerate(message):
            [(ref, held)] = [
                (ref, held)
                for ref, held in zip(sources, MAIN)
                if (j + shift, b) in held
            ]
            out_ref[k] = ref[held.index((j + shift, b))]


def placements():
    found = {}
    for operand, message in enumerate(ARRIVE):
        for k, (j, b) in enumerate(message):
            column = SLOT.get((j + OFFSETS[b]) % NBG)
            if column is not None:
                found[SLOT[j % NBG], column] = (operand, k if operand else (b, j))
    return found


def purify_body(me_ref, presence_ref, *refs):
    sources, outs = refs[: len(ARRIVE)], refs[len(ARRIVE) : len(ARRIVE) + LAYERS]
    right_ref, left_ref, result_ref = refs[len(ARRIVE) + LAYERS :]
    me = me_ref[0]
    placed = placements()
    zero = jnp.zeros((BS, BS), jnp.bfloat16)
    for row in range(16):
        for column in range(16):
            where = (pl.ds(row * BS, BS), pl.ds(column * BS, BS))
            if (row, column) in placed:
                operand, index = placed[row, column]
                right_ref[where] = sources[operand][index]
            else:
                right_ref[where] = zero
    targets = {
        (i, SLOT[(i + offset) % NBG]): d
        for i in range(2)
        for d, offset in enumerate(OFFSETS)
    }
    for i in range(2):
        for column in range(16):
            where = (pl.ds(i * BS, BS), pl.ds(column * BS, BS))
            d = targets.get((i, column))
            left_ref[where] = zero if d is None else sources[0][d, i]

    def dot(left, right):
        return jnp.dot(left, right, preferred_element_type=jnp.float32)

    def product(columns):
        start = columns[0] * BS
        wide = pl.ds(start, len(columns) * BS)
        if start < NEAR_END:
            return dot(left_ref[...], right_ref[:, wide])
        if start < PLUS_END:
            return dot(left_ref[:, :PLUS_END], right_ref[:PLUS_END, wide])
        return dot(left_ref[:, :NEAR_END], right_ref[:NEAR_END, wide]) + dot(
            left_ref[:, PLUS_END:], right_ref[PLUS_END:, wide]
        )

    def each(columns, total, use):
        for at, column in enumerate(columns):
            for i in range(2):
                d = targets.get((i, column))
                if d is not None:
                    tile = total[i * BS : (i + 1) * BS, at * BS : (at + 1) * BS]
                    use(i, column, d, presence_ref[d, 2 * me + i] != 0, tile)

    groups = [[c, c + 1] for c in range(0, 16, 2)]

    def keep_second(i, column, d, present, tile):
        second = jnp.where(present, tile, jnp.zeros_like(tile)).astype(jnp.bfloat16)
        result_ref[d, i] = second

    for columns in groups:
        each(columns, product(columns), keep_second)
    for (i, column), d in targets.items():
        left_ref[pl.ds(i * BS, BS), pl.ds(column * BS, BS)] = result_ref[d, i]

    def keep_result(i, column, d, present, tile):
        third = jnp.where(present, tile, jnp.zeros_like(tile))
        second = result_ref[d, i].astype(jnp.float32)
        result_ref[d, i] = (3.0 * second - 2.0 * third).astype(jnp.bfloat16)

    for columns in groups:
        each(columns, product(columns), keep_result)
    for s, out_ref in enumerate(outs):
        other = lax.rem(me - s + LAYERS, LAYERS)
        start = pl.multiple_of(other * (BS // LAYERS), BS // LAYERS)
        out_ref[...] = result_ref[:, :, pl.ds(start, BS // LAYERS), :]


def join_body(me_ref, *refs):
    me = me_ref[0]
    out_ref = refs[LAYERS]
    for s in range(LAYERS):
        row = 2 * lax.rem(me + s, LAYERS)
        for t in range(2):
            for d in range(DIAGS):
                out_ref[d, row + t] = refs[s][d, t]


def exchanged(pieces):
    far = from_layer(pieces[2], 2)
    return [pieces[0], from_layer(pieces[1], 1), far, from_layer(pieces[3], 3)]


def per_device(blocks, presence):
    me = lax.axis_index("layer").astype(jnp.int32).reshape(1)

    def packed(messages):
        return [bf16(len(message), BS, BS) for message in messages]

    quarter = bf16(DIAGS, 2, BS // LAYERS, BS)
    shared_quarter = bf16(len(SHARED), 2, BS // LAYERS, BS)
    *pieces, shared = call(
        split_body,
        [quarter] * LAYERS + [bf16(len(SHARED), 2 * LAYERS, BS // LAYERS, BS)],
        2,
        1,
    )(me, presence, blocks)
    shared = swapped(shared)
    pieces = exchanged(pieces)
    own, plus_far, minus_far, lower, higher = call(
        functools.partial(pack_body, DIRECT + NEAR[2:]),
        [bf16(DIAGS, 2, BS, BS)] + packed(DIRECT + NEAR[2:]),
        1,
        LAYERS,
    )(me, *pieces)
    plus_far = from_pair(plus_far, FAR_PAIRS)
    minus_far = from_pair(minus_far, -FAR_PAIRS)
    lower, higher = from_pair(lower, -2), from_pair(higher, 2)
    some = [shared, own]
    some = call(resplit_body, [shared_quarter] * LAYERS, 1, len(some))(me, *some)
    some = exchanged(some)
    band = call(fan_body, packed([FAN])[0], 1, LAYERS)(me, *some)
    plus_band, minus_band = far_across(band, FAR_PAIRS), far_across(band, -FAR_PAIRS)
    before = [own, band]
    before += [lower, higher]
    low, high = call(near_body, packed(NEAR[:2]), 0, len(before))(*before)
    low, high = from_pair(low, -1), from_pair(high, 1)
    arrived = [plus_far, minus_far, plus_band, minus_band]
    edge_low, edge_high = call(
        edge_body, packed([EDGE_LOW, EDGE_HIGH]), 0, len(arrived)
    )(*arrived)
    edge_low, edge_high = from_pair(edge_low, -1), from_pair(edge_high, 1)
    results = call(
        purify_body,
        [quarter] * LAYERS,
        2,
        len(ARRIVE),
        scratch=[
            pltpu.VMEM((WIDTH, WIDTH), jnp.bfloat16),
            pltpu.VMEM((2 * BS, WIDTH), jnp.bfloat16),
            pltpu.VMEM((DIAGS, 2, BS, BS), jnp.bfloat16),
        ],
        flops=4 * 224 * 2 * BS**3,
    )(me, presence, own, low, high, lower, higher, *arrived, edge_low, edge_high)
    results = exchanged(results)
    return call(join_body, bf16(DIAGS, 2 * LAYERS, BS // LAYERS, BS), 1, LAYERS)(
        me, *results
    )


def solution(mesh):
    placed = (P(None, ("row", "col"), "layer", None), P(None, ("row", "col")))
    return jax.shard_map(
        per_device,
        mesh=mesh,
        in_specs=placed,
        out_specs=P(None, ("row", "col"), "layer", None),
        check_vma=False,
    )
```

```python
import functools

import jax
import jax.numpy as jnp
from jax import lax
from jax.experimental import pallas as pl
from jax.experimental.pallas import tpu as pltpu
from jax.sharding import PartitionSpec as P

NBG = 512
BAND = 3
FAR = 160
BS = 128
LAYERS = 4
PAIRS = NBG // 2
FAR_PAIRS = FAR // 2
AXES = ("layer", "row", "col")
OFFSETS = list(range(-BAND, BAND + 1)) + [
    FAR - 1, FAR, FAR + 1, -FAR - 1, -FAR, -FAR + 1,
]
DIAGS = len(OFFSETS)
OFFSET_SET = {value % NBG for value in OFFSETS}

REACH = (
    list(range(-BAND, BAND + 2))
    + list(range(FAR - 1, FAR + 3))
    + list(range(-FAR - 1, -FAR + 3))
)
SLOT = {value % NBG: index for index, value in enumerate(REACH)}
NEAR_END = 8 * BS
PLUS_END = 12 * BS
WIDTH = 16 * BS


def needed(j):
    found = set()
    for i in range(2):
        for left in OFFSETS:
            if (i + left - j) % NBG == 0:
                for b, right in enumerate(OFFSETS):
                    if (left + right) % NBG in OFFSET_SET:
                        found.add(b)
    return sorted(found)


BANDS = range(2 * BAND + 1)
SHARED = sorted(b for b in set().union(*(needed(FAR + t) for t in range(-1, 3))) if b in BANDS)


def band_of(j):
    return [b for b in needed(j) if b in BANDS]


def far_of(j):
    return [b for b in needed(j) if b not in BANDS]


def tiles(rows, which=needed):
    return [(j, b) for j in rows for b in which(j)]


OWN = [(t, b) for b in range(DIAGS) for t in range(2)]
LOW, HIGH = tiles([-2, -1]), tiles([2, 3])
LOWER, HIGHER = tiles([-3]), tiles([4])
FAN = [(FAR + t, b) for t in range(2) for b in SHARED]
PLUS_BAND = FAN
MINUS_BAND = [(j - 2 * FAR, b) for j, b in FAN]
PLUS_FAR = tiles([FAR, FAR + 1], far_of)
MINUS_FAR = tiles([-FAR, -FAR + 1], far_of)
EDGE_LOW = tiles([FAR - 1, -FAR - 1])
EDGE_HIGH = tiles([FAR + 2, -FAR + 2])
MAIN = [PLUS_FAR, MINUS_FAR, PLUS_BAND, MINUS_BAND]
ARRIVE = [OWN, LOW, HIGH, LOWER, HIGHER] + MAIN + [EDGE_LOW, EDGE_HIGH]
NEAR = [[(j % 2, b) for j, b in message] for message in (LOW, HIGH, LOWER, HIGHER)]
DIRECT = [[(j % 2, b) for j, b in message] for message in (PLUS_FAR, MINUS_FAR)]


def place_of(p):
    return p % LAYERS * (PAIRS // LAYERS) + p // LAYERS


def moved(x, source_of):
    route = [(place_of(source_of(p)), place_of(p)) for p in range(PAIRS)]
    return lax.ppermute(x, AXES, route)


def across(p):
    cols = LAYERS * 8
    return p - p % cols + (p + cols // 2) % cols


def from_pair(x, distance):
    return moved(x, lambda p: (p + distance) % PAIRS)


def same_group(p, distance):
    return p - p % LAYERS + (p + distance) % LAYERS


def from_layer(x, distance):
    return moved(x, lambda p: same_group(p, distance))


def swapped(x):
    return moved(x, across)


def far_across(x, distance):
    return moved(x, lambda p: across((p + distance) % PAIRS))


def bf16(*shape):
    return jax.ShapeDtypeStruct(shape, jnp.bfloat16)


def call(body, out_shape, n_smem, n_vmem, scratch=(), flops=0, traffic=1 << 22):
    in_specs = [pl.BlockSpec(memory_space=pltpu.SMEM)] * n_smem
    in_specs += [pl.BlockSpec(memory_space=pltpu.VMEM)] * n_vmem
    return pl.pallas_call(
        body,
        out_shape=out_shape,
        in_specs=in_specs,
        out_specs=jax.tree.map(
            lambda _: pl.BlockSpec(memory_space=pltpu.VMEM), out_shape
        ),
        scratch_shapes=list(scratch),
        compiler_params=pltpu.CompilerParams(vmem_limit_bytes=48 << 20),
        cost_estimate=pl.CostEstimate(
            flops=flops, bytes_accessed=traffic, transcendentals=0
        ),
    )


def split_body(me_ref, presence_ref, blocks_ref, *out_refs):
    me = me_ref[0]
    shared_ref = out_refs[LAYERS]
    for s in range(LAYERS):
        other = lax.rem(me - s + LAYERS, LAYERS)
        for t in range(2):
            row = 2 * other + t
            for d in range(DIAGS):
                tile = blocks_ref[d, row]
                present = presence_ref[d, row] != 0
                tile = jnp.where(present, tile, jnp.zeros_like(tile))
                out_refs[s][d, t] = tile
                if d in SHARED:
                    shared_ref[SHARED.index(d), row] = tile


def resplit_body(me_ref, shared_ref, *out_refs):
    for s, out_ref in enumerate(out_refs[-LAYERS:]):
        row = 2 * lax.rem(me_ref[0] - s + LAYERS, LAYERS)
        for t in range(2):
            for k in range(len(SHARED)):
                out_ref[k, t] = shared_ref[k, row + t]


def gather_pieces(me, pieces, out_ref):
    for s, piece in enumerate(pieces):
        other = lax.rem(me + s, LAYERS)
        start = pl.multiple_of(other * (BS // LAYERS), BS // LAYERS)
        out_ref[:, :, pl.ds(start, BS // LAYERS), :] = piece[...]


def pack_body(messages, me_ref, *refs):
    pieces, own_ref, out_refs = refs[:LAYERS], refs[LAYERS], refs[LAYERS + 1 :]
    gather_pieces(me_ref[0], pieces, own_ref)
    for message, out_ref in zip(messages, out_refs):
        for k, (t, b) in enumerate(message):
            out_ref[k] = own_ref[b, t]


def near_body(own_ref, *refs):
    for message, out_ref in zip(NEAR[:2], refs[-2:]):
        for k, (t, b) in enumerate(message):
            out_ref[k] = own_ref[b, t]


def fan_body(me_ref, *refs):
    pieces, out_ref = refs[:LAYERS], refs[LAYERS]
    for s, piece in enumerate(pieces):
        other = lax.rem(me_ref[0] + s, LAYERS)
        rows = pl.ds(pl.multiple_of(other * (BS // LAYERS), BS // LAYERS), BS // LAYERS)
        for k, (j, b) in enumerate(FAN):
            out_ref[k, rows, :] = piece[SHARED.index(b), j - FAR]


def edge_body(*refs):
    sources, out_refs = refs[: len(MAIN)], refs[len(MAIN) :]
    for shift, message, out_ref in zip((2, -2), (EDGE_LOW, EDGE_HIGH), out_refs):
        for k, (j, b) in enumerate(message):
            [(ref, held)] = [
                (ref, held)
                for ref, held in zip(sources, MAIN)
                if (j + shift, b) in held
            ]
            out_ref[k] = ref[held.index((j + shift, b))]


def placements():
    found = {}
    for operand, message in enumerate(ARRIVE):
        for k, (j, b) in enumerate(message):
            column = SLOT.get((j + OFFSETS[b]) % NBG)
            if column is not None:
                found[SLOT[j % NBG], column] = (operand, k if operand else (b, j))
    return found


def purify_body(me_ref, presence_ref, *refs):
    sources, outs = refs[: len(ARRIVE)], refs[len(ARRIVE) : len(ARRIVE) + LAYERS]
    right_ref, left_ref, result_ref = refs[len(ARRIVE) + LAYERS :]
    me = me_ref[0]
    placed = placements()
    zero = jnp.zeros((BS, BS), jnp.bfloat16)
    for row in range(16):
        for column in range(16):
            where = (pl.ds(row * BS, BS), pl.ds(column * BS, BS))
            if (row, column) in placed:
                operand, index = placed[row, column]
                right_ref[where] = sources[operand][index]
            else:
                right_ref[where] = zero
    targets = {
        (i, SLOT[(i + offset) % NBG]): d
        for i in range(2)
        for d, offset in enumerate(OFFSETS)
    }
    for i in range(2):
        for column in range(16):
            where = (pl.ds(i * BS, BS), pl.ds(column * BS, BS))
            d = targets.get((i, column))
            left_ref[where] = zero if d is None else sources[0][d, i]

    def dot(left, right):
        return jnp.dot(left, right, preferred_element_type=jnp.float32)

    def product(columns):
        start = columns[0] * BS
        wide = pl.ds(start, len(columns) * BS)
        if start < NEAR_END:
            return dot(left_ref[...], right_ref[:, wide])
        if start < PLUS_END:
            return dot(left_ref[:, :PLUS_END], right_ref[:PLUS_END, wide])
        return dot(left_ref[:, :NEAR_END], right_ref[:NEAR_END, wide]) + dot(
            left_ref[:, PLUS_END:], right_ref[PLUS_END:, wide]
        )

    def each(columns, total, use):
        for at, column in enumerate(columns):
            for i in range(2):
                d = targets.get((i, column))
                if d is not None:
                    tile = total[i * BS : (i + 1) * BS, at * BS : (at + 1) * BS]
                    use(i, column, d, presence_ref[d, 2 * me + i] != 0, tile)

    groups = [[c, c + 1] for c in range(0, 16, 2)]

    def keep_second(i, column, d, present, tile):
        second = jnp.where(present, tile, jnp.zeros_like(tile)).astype(jnp.bfloat16)
        result_ref[d, i] = second

    for columns in groups:
        each(columns, product(columns), keep_second)
    for (i, column), d in targets.items():
        left_ref[pl.ds(i * BS, BS), pl.ds(column * BS, BS)] = result_ref[d, i]

    def keep_result(i, column, d, present, tile):
        third = jnp.where(present, tile, jnp.zeros_like(tile))
        second = result_ref[d, i].astype(jnp.float32)
        result_ref[d, i] = (3.0 * second - 2.0 * third).astype(jnp.bfloat16)

    for columns in groups:
        each(columns, product(columns), keep_result)
    for s, out_ref in enumerate(outs):
        other = lax.rem(me - s + LAYERS, LAYERS)
        start = pl.multiple_of(other * (BS // LAYERS), BS // LAYERS)
        out_ref[...] = result_ref[:, :, pl.ds(start, BS // LAYERS), :]


def join_body(me_ref, *refs):
    me = me_ref[0]
    out_ref = refs[LAYERS]
    for s in range(LAYERS):
        row = 2 * lax.rem(me + s, LAYERS)
        for t in range(2):
            for d in range(DIAGS):
                out_ref[d, row + t] = refs[s][d, t]


def exchanged(pieces):
    far = from_layer(pieces[2], 2)
    return [pieces[0], from_layer(pieces[1], 1), far, from_layer(pieces[3], 3)]


def per_device(blocks, presence):
    me = lax.axis_index("layer").astype(jnp.int32).reshape(1)

    def packed(messages):
        return [bf16(len(message), BS, BS) for message in messages]

    quarter = bf16(DIAGS, 2, BS // LAYERS, BS)
    shared_quarter = bf16(len(SHARED), 2, BS // LAYERS, BS)
    *pieces, shared = call(
        split_body,
        [quarter] * LAYERS + [bf16(len(SHARED), 2 * LAYERS, BS // LAYERS, BS)],
        2,
        1,
    )(me, presence, blocks)
    shared = swapped(shared)
    pieces = exchanged(pieces)
    own, plus_far, minus_far, lower, higher = call(
        functools.partial(pack_body, DIRECT + NEAR[2:]),
        [bf16(DIAGS, 2, BS, BS)] + packed(DIRECT + NEAR[2:]),
        1,
        LAYERS,
    )(me, *pieces)
    plus_far = from_pair(plus_far, FAR_PAIRS)
    minus_far = from_pair(minus_far, -FAR_PAIRS)
    lower, higher = from_pair(lower, -2), from_pair(higher, 2)
    some = [shared, own]
    some = call(resplit_body, [shared_quarter] * LAYERS, 1, len(some))(me, *some)
    some = exchanged(some)
    band = call(fan_body, packed([FAN])[0], 1, LAYERS)(me, *some)
    plus_band, minus_band = far_across(band, FAR_PAIRS), far_across(band, -FAR_PAIRS)
    before = [own, band]
    before += [lower, higher]
    before += [plus_far, minus_far]
    low, high = call(near_body, packed(NEAR[:2]), 0, len(before))(*before)
    low, high = from_pair(low, -1), from_pair(high, 1)
    arrived = [plus_far, minus_far, plus_band, minus_band]
    edge_low, edge_high = call(
        edge_body, packed([EDGE_LOW, EDGE_HIGH]), 0, len(arrived)
    )(*arrived)
    edge_low, edge_high = from_pair(edge_low, -1), from_pair(edge_high, 1)
    results = call(
        purify_body,
        [quarter] * LAYERS,
        2,
        len(ARRIVE),
        scratch=[
            pltpu.VMEM((WIDTH, WIDTH), jnp.bfloat16),
            pltpu.VMEM((2 * BS, WIDTH), jnp.bfloat16),
            pltpu.VMEM((DIAGS, 2, BS, BS), jnp.bfloat16),
        ],
        flops=4 * 224 * 2 * BS**3,
    )(me, presence, own, low, high, lower, higher, *arrived, edge_low, edge_high)
    results = exchanged(results)
    return call(join_body, bf16(DIAGS, 2 * LAYERS, BS // LAYERS, BS), 1, LAYERS)(
        me, *results
    )


def solution(mesh):
    placed = (P(None, ("row", "col"), "layer", None), P(None, ("row", "col")))
    return jax.shard_map(
        per_device,
        mesh=mesh,
        in_specs=placed,
        out_specs=P(None, ("row", "col"), "layer", None),
        check_vma=False,
    )
```

```python
import functools

import jax
import jax.numpy as jnp
from jax import lax
from jax.experimental import pallas as pl
from jax.experimental.pallas import tpu as pltpu
from jax.sharding import PartitionSpec as P

NBG = 512
BAND = 3
FAR = 160
BS = 128
LAYERS = 4
PAIRS = NBG // 2
FAR_PAIRS = FAR // 2
AXES = ("layer", "row", "col")
OFFSETS = list(range(-BAND, BAND + 1)) + [
    FAR - 1, FAR, FAR + 1, -FAR - 1, -FAR, -FAR + 1,
]
DIAGS = len(OFFSETS)
OFFSET_SET = {value % NBG for value in OFFSETS}

REACH = (
    list(range(-BAND, BAND + 2))
    + list(range(FAR - 1, FAR + 3))
    + list(range(-FAR - 1, -FAR + 3))
)
SLOT = {value % NBG: index for index, value in enumerate(REACH)}
NEAR_END = 8 * BS
PLUS_END = 12 * BS
WIDTH = 16 * BS


def needed(j):
    found = set()
    for i in range(2):
        for left in OFFSETS:
            if (i + left - j) % NBG == 0:
                for b, right in enumerate(OFFSETS):
                    if (left + right) % NBG in OFFSET_SET:
                        found.add(b)
    return sorted(found)


BANDS = range(2 * BAND + 1)
SHARED = sorted(b for b in set().union(*(needed(FAR + t) for t in range(-1, 3))) if b in BANDS)


def band_of(j):
    return [b for b in needed(j) if b in BANDS]


def far_of(j):
    return [b for b in needed(j) if b not in BANDS]


def tiles(rows, which=needed):
    return [(j, b) for j in rows for b in which(j)]


OWN = [(t, b) for b in range(DIAGS) for t in range(2)]
LOW, HIGH = tiles([-2, -1]), tiles([2, 3])
LOWER, HIGHER = tiles([-3]), tiles([4])
FAN = [(FAR + t, b) for t in range(2) for b in SHARED]
PLUS_BAND = FAN
MINUS_BAND = [(j - 2 * FAR, b) for j, b in FAN]
PLUS_FAR = tiles([FAR, FAR + 1], far_of)
MINUS_FAR = tiles([-FAR, -FAR + 1], far_of)
EDGE_LOW = tiles([FAR - 1, -FAR - 1])
EDGE_HIGH = tiles([FAR + 2, -FAR + 2])
MAIN = [PLUS_FAR, MINUS_FAR, PLUS_BAND, MINUS_BAND]
ARRIVE = [OWN, LOW, HIGH, LOWER, HIGHER] + MAIN + [EDGE_LOW, EDGE_HIGH]
NEAR = [[(j % 2, b) for j, b in message] for message in (LOW, HIGH, LOWER, HIGHER)]
DIRECT = [[(j % 2, b) for j, b in message] for message in (PLUS_FAR, MINUS_FAR)]


def place_of(p):
    return p % LAYERS * (PAIRS // LAYERS) + p // LAYERS


def moved(x, source_of):
    route = [(place_of(source_of(p)), place_of(p)) for p in range(PAIRS)]
    return lax.ppermute(x, AXES, route)


def across(p):
    cols = LAYERS * 8
    return p - p % cols + (p + cols // 2) % cols


def from_pair(x, distance):
    return moved(x, lambda p: (p + distance) % PAIRS)


def same_group(p, distance):
    return p - p % LAYERS + (p + distance) % LAYERS


def from_layer(x, distance):
    return moved(x, lambda p: same_group(p, distance))


def swapped(x):
    return moved(x, across)


def far_across(x, distance):
    return moved(x, lambda p: across((p + distance) % PAIRS))


def bf16(*shape):
    return jax.ShapeDtypeStruct(shape, jnp.bfloat16)


def call(body, out_shape, n_smem, n_vmem, scratch=(), flops=0, traffic=1 << 22):
    in_specs = [pl.BlockSpec(memory_space=pltpu.SMEM)] * n_smem
    in_specs += [pl.BlockSpec(memory_space=pltpu.VMEM)] * n_vmem
    return pl.pallas_call(
        body,
        out_shape=out_shape,
        in_specs=in_specs,
        out_specs=jax.tree.map(
            lambda _: pl.BlockSpec(memory_space=pltpu.VMEM), out_shape
        ),
        scratch_shapes=list(scratch),
        compiler_params=pltpu.CompilerParams(vmem_limit_bytes=48 << 20),
        cost_estimate=pl.CostEstimate(
            flops=flops, bytes_accessed=traffic, transcendentals=0
        ),
    )


def split_body(me_ref, presence_ref, blocks_ref, *out_refs):
    me = me_ref[0]
    shared_ref = out_refs[LAYERS]
    for s in range(LAYERS):
        other = lax.rem(me - s + LAYERS, LAYERS)
        for t in range(2):
            row = 2 * other + t
            for d in range(DIAGS):
                tile = blocks_ref[d, row]
                present = presence_ref[row, d] != 0
                tile = jnp.where(present, tile, jnp.zeros_like(tile))
                out_refs[s][d, t] = tile
                if d in SHARED:
                    shared_ref[SHARED.index(d), row] = tile


def resplit_body(me_ref, shared_ref, *out_refs):
    for s, out_ref in enumerate(out_refs[-LAYERS:]):
        row = 2 * lax.rem(me_ref[0] - s + LAYERS, LAYERS)
        for t in range(2):
            for k in range(len(SHARED)):
                out_ref[k, t] = shared_ref[k, row + t]


def gather_pieces(me, pieces, out_ref):
    for s, piece in enumerate(pieces):
        other = lax.rem(me + s, LAYERS)
        start = pl.multiple_of(other * (BS // LAYERS), BS // LAYERS)
        out_ref[:, :, pl.ds(start, BS // LAYERS), :] = piece[...]


def pack_body(messages, me_ref, *refs):
    pieces, own_ref, out_refs = refs[:LAYERS], refs[LAYERS], refs[LAYERS + 1 :]
    gather_pieces(me_ref[0], pieces, own_ref)
    for message, out_ref in zip(messages, out_refs):
        for k, (t, b) in enumerate(message):
            out_ref[k] = own_ref[b, t]


def near_body(own_ref, *refs):
    for message, out_ref in zip(NEAR[:2], refs[-2:]):
        for k, (t, b) in enumerate(message):
            out_ref[k] = own_ref[b, t]


def fan_body(me_ref, *refs):
    pieces, out_ref = refs[:LAYERS], refs[-1]
    for s, piece in enumerate(pieces):
        other = lax.rem(me_ref[0] + s, LAYERS)
        rows = pl.ds(pl.multiple_of(other * (BS // LAYERS), BS // LAYERS), BS // LAYERS)
        for k, (j, b) in enumerate(FAN):
            out_ref[k, rows, :] = piece[SHARED.index(b), j - FAR]


def edge_body(*refs):
    sources, out_refs = refs[: len(MAIN)], refs[len(MAIN) :]
    for shift, message, out_ref in zip((2, -2), (EDGE_LOW, EDGE_HIGH), out_refs):
        for k, (j, b) in enumerate(message):
            [(ref, held)] = [
                (ref, held)
                for ref, held in zip(sources, MAIN)
                if (j + shift, b) in held
            ]
            out_ref[k] = ref[held.index((j + shift, b))]


def placements():
    found = {}
    for operand, message in enumerate(ARRIVE):
        for k, (j, b) in enumerate(message):
            column = SLOT.get((j + OFFSETS[b]) % NBG)
            if column is not None:
                found[SLOT[j % NBG], column] = (operand, k if operand else (b, j))
    return found


def purify_body(me_ref, presence_ref, *refs):
    sources, outs = refs[: len(ARRIVE)], refs[len(ARRIVE) : len(ARRIVE) + LAYERS]
    right_ref, left_ref, result_ref = refs[len(ARRIVE) + LAYERS :]
    me = me_ref[0]
    placed = placements()
    zero = jnp.zeros((BS, BS), jnp.bfloat16)
    for row in range(16):
        for column in range(16):
            where = (pl.ds(row * BS, BS), pl.ds(column * BS, BS))
            if (row, column) in placed:
                operand, index = placed[row, column]
                right_ref[where] = sources[operand][index]
            else:
                right_ref[where] = zero
    targets = {
        (i, SLOT[(i + offset) % NBG]): d
        for i in range(2)
        for d, offset in enumerate(OFFSETS)
    }
    for i in range(2):
        for column in range(16):
            where = (pl.ds(i * BS, BS), pl.ds(column * BS, BS))
            d = targets.get((i, column))
            left_ref[where] = zero if d is None else sources[0][d, i]

    def dot(left, right):
        return jnp.dot(left, right, preferred_element_type=jnp.float32)

    def product(columns):
        start = columns[0] * BS
        wide = pl.ds(start, len(columns) * BS)
        if start < NEAR_END:
            return dot(left_ref[...], right_ref[:, wide])
        if start < PLUS_END:
            return dot(left_ref[:, :PLUS_END], right_ref[:PLUS_END, wide])
        return dot(left_ref[:, :NEAR_END], right_ref[:NEAR_END, wide]) + dot(
            left_ref[:, PLUS_END:], right_ref[PLUS_END:, wide]
        )

    def each(columns, total, use):
        for at, column in enumerate(columns):
            for i in range(2):
                d = targets.get((i, column))
                if d is not None:
                    tile = total[i * BS : (i + 1) * BS, at * BS : (at + 1) * BS]
                    use(i, column, d, presence_ref[2 * me + i, d] != 0, tile)

    groups = [[c, c + 1] for c in range(0, 16, 2)]

    def keep_second(i, column, d, present, tile):
        second = jnp.where(present, tile, jnp.zeros_like(tile)).astype(jnp.bfloat16)
        result_ref[d, i] = second

    for columns in groups:
        each(columns, product(columns), keep_second)
    for (i, column), d in targets.items():
        left_ref[pl.ds(i * BS, BS), pl.ds(column * BS, BS)] = result_ref[d, i]

    def keep_result(i, column, d, present, tile):
        third = jnp.where(present, tile, jnp.zeros_like(tile))
        second = result_ref[d, i].astype(jnp.float32)
        result_ref[d, i] = (3.0 * second - 2.0 * third).astype(jnp.bfloat16)

    for columns in groups:
        each(columns, product(columns), keep_result)
    for s, out_ref in enumerate(outs):
        other = lax.rem(me - s + LAYERS, LAYERS)
        start = pl.multiple_of(other * (BS // LAYERS), BS // LAYERS)
        out_ref[...] = result_ref[:, :, pl.ds(start, BS // LAYERS), :]


def join_body(me_ref, *refs):
    me = me_ref[0]
    out_ref = refs[LAYERS]
    for s in range(LAYERS):
        row = 2 * lax.rem(me + s, LAYERS)
        for t in range(2):
            for d in range(DIAGS):
                out_ref[d, row + t] = refs[s][d, t]


def exchanged(pieces):
    far = from_layer(pieces[2], 2)
    return [pieces[0], from_layer(pieces[1], 1), far, from_layer(pieces[3], 3)]


def per_device(blocks, presence):
    me = lax.axis_index("layer").astype(jnp.int32).reshape(1)
    presence = presence.T

    def packed(messages):
        return [bf16(len(message), BS, BS) for message in messages]

    quarter = bf16(DIAGS, 2, BS // LAYERS, BS)
    shared_quarter = bf16(len(SHARED), 2, BS // LAYERS, BS)
    *pieces, shared = call(
        split_body,
        [quarter] * LAYERS + [bf16(len(SHARED), 2 * LAYERS, BS // LAYERS, BS)],
        2,
        1,
    )(me, presence, blocks)
    shared = swapped(shared)
    pieces = exchanged(pieces)
    own, plus_far, minus_far, lower, higher = call(
        functools.partial(pack_body, DIRECT + NEAR[2:]),
        [bf16(DIAGS, 2, BS, BS)] + packed(DIRECT + NEAR[2:]),
        1,
        LAYERS,
    )(me, *pieces)
    plus_far = from_pair(plus_far, FAR_PAIRS)
    minus_far = from_pair(minus_far, -FAR_PAIRS)
    lower, higher = from_pair(lower, -2), from_pair(higher, 2)
    some = [shared, own]
    some = call(resplit_body, [shared_quarter] * LAYERS, 1, len(some))(me, *some)
    some = exchanged(some)
    band = call(fan_body, packed([FAN])[0], 1, LAYERS + 2)(me, *some, lower, higher)
    plus_band, minus_band = far_across(band, FAR_PAIRS), far_across(band, -FAR_PAIRS)
    before = [own]
    before += [plus_far, minus_far]
    low, high = call(near_body, packed(NEAR[:2]), 0, len(before))(*before)
    low, high = from_pair(low, -1), from_pair(high, 1)
    arrived = [plus_far, minus_far, plus_band, minus_band]
    edge_low, edge_high = call(
        edge_body, packed([EDGE_LOW, EDGE_HIGH]), 0, len(arrived)
    )(*arrived)
    edge_low, edge_high = from_pair(edge_low, -1), from_pair(edge_high, 1)
    results = call(
        purify_body,
        [quarter] * LAYERS,
        2,
        len(ARRIVE),
        scratch=[
            pltpu.VMEM((WIDTH, WIDTH), jnp.bfloat16),
            pltpu.VMEM((2 * BS, WIDTH), jnp.bfloat16),
            pltpu.VMEM((DIAGS, 2, BS, BS), jnp.bfloat16),
        ],
        flops=4 * 224 * 2 * BS**3,
    )(me, presence, own, low, high, lower, higher, *arrived, edge_low, edge_high)
    results = exchanged(results)
    return call(join_body, bf16(DIAGS, 2 * LAYERS, BS // LAYERS, BS), 1, LAYERS)(
        me, *results
    )


def solution(mesh):
    placed = (P(None, ("row", "col"), "layer", None), P(None, ("row", "col")))
    return jax.shard_map(
        per_device,
        mesh=mesh,
        in_specs=placed,
        out_specs=P(None, ("row", "col"), "layer", None),
        check_vma=False,
    )
```

```python
import functools

import jax
import jax.numpy as jnp
from jax import lax
from jax.experimental import pallas as pl
from jax.experimental.pallas import tpu as pltpu
from jax.sharding import PartitionSpec as P

NBG = 512
BAND = 3
FAR = 160
BS = 128
LAYERS = 4
PAIRS = NBG // 2
FAR_PAIRS = FAR // 2
AXES = ("layer", "row", "col")
OFFSETS = list(range(-BAND, BAND + 1)) + [
    FAR - 1, FAR, FAR + 1, -FAR - 1, -FAR, -FAR + 1,
]
DIAGS = len(OFFSETS)
OFFSET_SET = {value % NBG for value in OFFSETS}

REACH = (
    list(range(-BAND, BAND + 2))
    + list(range(FAR - 1, FAR + 3))
    + list(range(-FAR - 1, -FAR + 3))
)
SLOT = {value % NBG: index for index, value in enumerate(REACH)}
NEAR_END = 8 * BS
PLUS_END = 12 * BS
WIDTH = 16 * BS


def needed(j):
    found = set()
    for i in range(2):
        for left in OFFSETS:
            if (i + left - j) % NBG == 0:
                for b, right in enumerate(OFFSETS):
                    if (left + right) % NBG in OFFSET_SET:
                        found.add(b)
    return sorted(found)


BANDS = range(2 * BAND + 1)
SHARED = sorted(b for b in set().union(*(needed(FAR + t) for t in range(-1, 3))) if b in BANDS)


def band_of(j):
    return [b for b in needed(j) if b in BANDS]


def far_of(j):
    return [b for b in needed(j) if b not in BANDS]


def tiles(rows, which=needed):
    return [(j, b) for j in rows for b in which(j)]


OWN = [(t, b) for b in range(DIAGS) for t in range(2)]
LOW, HIGH = tiles([-2, -1]), tiles([2, 3])
LOWER, HIGHER = tiles([-3]), tiles([4])
FAN = [(FAR + t, b) for t in range(2) for b in SHARED]
PLUS_BAND = FAN
MINUS_BAND = [(j - 2 * FAR, b) for j, b in FAN]
PLUS_FAR = tiles([FAR, FAR + 1], far_of)
MINUS_FAR = tiles([-FAR, -FAR + 1], far_of)
EDGE_LOW = tiles([FAR - 1, -FAR - 1])
EDGE_HIGH = tiles([FAR + 2, -FAR + 2])
MAIN = [PLUS_FAR, MINUS_FAR, PLUS_BAND, MINUS_BAND]
ARRIVE = [OWN, LOW, HIGH, LOWER, HIGHER] + MAIN + [EDGE_LOW, EDGE_HIGH]
NEAR = [[(j % 2, b) for j, b in message] for message in (LOW, HIGH, LOWER, HIGHER)]
DIRECT = [[(j % 2, b) for j, b in message] for message in (PLUS_FAR, MINUS_FAR)]


def place_of(p):
    return p % LAYERS * (PAIRS // LAYERS) + p // LAYERS


def moved(x, source_of):
    route = [(place_of(source_of(p)), place_of(p)) for p in range(PAIRS)]
    return lax.ppermute(x, AXES, route)


def across(p):
    cols = LAYERS * 8
    return p - p % cols + (p + cols // 2) % cols


def from_pair(x, distance):
    return moved(x, lambda p: (p + distance) % PAIRS)


def same_group(p, distance):
    return p - p % LAYERS + (p + distance) % LAYERS


def from_layer(x, distance):
    return moved(x, lambda p: same_group(p, distance))


def swapped(x):
    return moved(x, across)


def far_across(x, distance):
    return moved(x, lambda p: across((p + distance) % PAIRS))


def bf16(*shape):
    return jax.ShapeDtypeStruct(shape, jnp.bfloat16)


def call(body, out_shape, n_smem, n_vmem, scratch=(), flops=0, traffic=1 << 22):
    in_specs = [pl.BlockSpec(memory_space=pltpu.SMEM)] * n_smem
    in_specs += [pl.BlockSpec(memory_space=pltpu.VMEM)] * n_vmem
    return pl.pallas_call(
        body,
        out_shape=out_shape,
        in_specs=in_specs,
        out_specs=jax.tree.map(
            lambda _: pl.BlockSpec(memory_space=pltpu.VMEM), out_shape
        ),
        scratch_shapes=list(scratch),
        compiler_params=pltpu.CompilerParams(vmem_limit_bytes=24 << 20),
        cost_estimate=pl.CostEstimate(
            flops=flops, bytes_accessed=traffic, transcendentals=0
        ),
    )


def split_body(me_ref, presence_ref, blocks_ref, *out_refs):
    me = me_ref[0]
    shared_ref = out_refs[LAYERS]
    for s in range(LAYERS):
        other = lax.rem(me - s + LAYERS, LAYERS)
        for t in range(2):
            row = 2 * other + t
            for d in range(DIAGS):
                tile = blocks_ref[d, row]
                present = presence_ref[d, row] != 0
                tile = jnp.where(present, tile, jnp.zeros_like(tile))
                out_refs[s][d, t] = tile
                if d in SHARED:
                    shared_ref[SHARED.index(d), row] = tile


def resplit_body(me_ref, shared_ref, *out_refs):
    for s, out_ref in enumerate(out_refs[-LAYERS:]):
        row = 2 * lax.rem(me_ref[0] - s + LAYERS, LAYERS)
        for t in range(2):
            for k in range(len(SHARED)):
                out_ref[k, t] = shared_ref[k, row + t]


def gather_pieces(me, pieces, out_ref):
    for s, piece in enumerate(pieces):
        other = lax.rem(me + s, LAYERS)
        start = pl.multiple_of(other * (BS // LAYERS), BS // LAYERS)
        out_ref[:, :, pl.ds(start, BS // LAYERS), :] = piece[...]


def pack_body(messages, me_ref, *refs):
    pieces, own_ref, out_refs = refs[:LAYERS], refs[LAYERS], refs[LAYERS + 1 :]
    gather_pieces(me_ref[0], pieces, own_ref)
    for message, out_ref in zip(messages, out_refs):
        for k, (t, b) in enumerate(message):
            out_ref[k] = own_ref[b, t]


def near_body(own_ref, *refs):
    for message, out_ref in zip(NEAR[:2], refs[-2:]):
        for k, (t, b) in enumerate(message):
            out_ref[k] = own_ref[b, t]


def fan_body(me_ref, *refs):
    pieces, out_ref = refs[:LAYERS], refs[LAYERS]
    for s, piece in enumerate(pieces):
        other = lax.rem(me_ref[0] + s, LAYERS)
        rows = pl.ds(pl.multiple_of(other * (BS // LAYERS), BS // LAYERS), BS // LAYERS)
        for k, (j, b) in enumerate(FAN):
            out_ref[k, rows, :] = piece[SHARED.index(b), j - FAR]


def edge_body(*refs):
    sources, out_refs = refs[: len(MAIN)], refs[len(MAIN) :]
    for shift, message, out_ref in zip((2, -2), (EDGE_LOW, EDGE_HIGH), out_refs):
        for k, (j, b) in enumerate(message):
            [(ref, held)] = [
                (ref, held)
                for ref, held in zip(sources, MAIN)
                if (j + shift, b) in held
            ]
            out_ref[k] = ref[held.index((j + shift, b))]


def placements():
    found = {}
    for operand, message in enumerate(ARRIVE):
        for k, (j, b) in enumerate(message):
            column = SLOT.get((j + OFFSETS[b]) % NBG)
            if column is not None:
                found[SLOT[j % NBG], column] = (operand, k if operand else (b, j))
    return found


NEAR_SOURCES = 5


def targets():
    return {
        (i, SLOT[(i + offset) % NBG]): d
        for i in range(2)
        for d, offset in enumerate(OFFSETS)
    }


def fill_right(out_ref, sources, first, rows):
    placed = placements()
    for row in rows:
        for column in range(16):
            where = (pl.ds((row - rows[0]) * BS, BS), pl.ds(column * BS, BS))
            if (row, column) in placed:
                operand, index = placed[row, column]
                out_ref[where] = sources[operand - first][index]
            else:
                out_ref[where] = jnp.zeros((BS, BS), jnp.bfloat16)


def fill_left(out_ref, own_ref, columns):
    for i in range(2):
        for column in columns:
            where = (pl.ds(i * BS, BS), pl.ds((column - columns[0]) * BS, BS))
            d = targets().get((i, column))
            if d is None:
                out_ref[where] = jnp.zeros((BS, BS), jnp.bfloat16)
            else:
                out_ref[where] = own_ref[d, i]


def dot(left, right):
    return jnp.dot(left, right, preferred_element_type=jnp.float32)


def near_product_body(*refs):
    sources, (right_ref, partial_ref, left_ref) = refs[:NEAR_SOURCES], refs[NEAR_SOURCES:]
    fill_right(right_ref, sources, 0, range(8))
    fill_left(left_ref, sources[0], range(8))
    for column in range(0, 16, 2):
        wide = pl.ds(column * BS, 2 * BS)
        partial_ref[:, wide] = dot(left_ref[...], right_ref[:, wide])


def purify_body(me_ref, presence_ref, own_ref, right_near_ref, partial_ref, *refs):
    fars = len(ARRIVE) - NEAR_SOURCES
    sources, outs = refs[:fars], refs[fars : fars + LAYERS]
    right_ref, left_ref, result_ref = refs[fars + LAYERS :]
    me = me_ref[0]
    fill_right(right_ref, sources, NEAR_SOURCES, range(8, 16))
    fill_left(left_ref, own_ref, range(16))

    def far_product(columns):
        start = columns[0] * BS
        wide = pl.ds(start, len(columns) * BS)
        if start < NEAR_END:
            return dot(left_ref[:, NEAR_END:], right_ref[:, wide])
        if start < PLUS_END:
            return dot(left_ref[:, NEAR_END:PLUS_END], right_ref[: PLUS_END - NEAR_END, wide])
        return dot(left_ref[:, PLUS_END:], right_ref[PLUS_END - NEAR_END :, wide])

    def near_product(columns):
        wide = pl.ds(columns[0] * BS, len(columns) * BS)
        return dot(left_ref[:, :NEAR_END], right_near_ref[:, wide])

    def each(columns, total, use):
        for at, column in enumerate(columns):
            for i in range(2):
                d = targets().get((i, column))
                if d is not None:
                    tile = total[i * BS : (i + 1) * BS, at * BS : (at + 1) * BS]
                    use(i, column, d, presence_ref[d, 2 * me + i] != 0, tile)

    groups = [[c, c + 1] for c in range(0, 16, 2)]

    def keep_second(i, column, d, present, tile):
        second = jnp.where(present, tile, jnp.zeros_like(tile)).astype(jnp.bfloat16)
        result_ref[d, i] = second

    for columns in groups:
        partial = partial_ref[:, pl.ds(columns[0] * BS, len(columns) * BS)]
        each(columns, partial + far_product(columns), keep_second)
    for (i, column), d in targets().items():
        left_ref[pl.ds(i * BS, BS), pl.ds(column * BS, BS)] = result_ref[d, i]

    def keep_result(i, column, d, present, tile):
        third = jnp.where(present, tile, jnp.zeros_like(tile))
        second = result_ref[d, i].astype(jnp.float32)
        result_ref[d, i] = (3.0 * second - 2.0 * third).astype(jnp.bfloat16)

    for columns in groups:
        each(columns, near_product(columns) + far_product(columns), keep_result)
    for s, out_ref in enumerate(outs):
        other = lax.rem(me - s + LAYERS, LAYERS)
        start = pl.multiple_of(other * (BS // LAYERS), BS // LAYERS)
        out_ref[...] = result_ref[:, :, pl.ds(start, BS // LAYERS), :]


def join_body(me_ref, *refs):
    me = me_ref[0]
    out_ref = refs[LAYERS]
    for s in range(LAYERS):
        row = 2 * lax.rem(me + s, LAYERS)
        for t in range(2):
            for d in range(DIAGS):
                out_ref[d, row + t] = refs[s][d, t]


def exchanged(pieces):
    far = from_layer(pieces[2], 2)
    return [pieces[0], from_layer(pieces[1], 1), far, from_layer(pieces[3], 3)]


def per_device(blocks, presence):
    me = lax.axis_index("layer").astype(jnp.int32).reshape(1)

    def packed(messages):
        return [bf16(len(message), BS, BS) for message in messages]

    quarter = bf16(DIAGS, 2, BS // LAYERS, BS)
    shared_quarter = bf16(len(SHARED), 2, BS // LAYERS, BS)
    *pieces, shared = call(
        split_body,
        [quarter] * LAYERS + [bf16(len(SHARED), 2 * LAYERS, BS // LAYERS, BS)],
        2,
        1,
    )(me, presence, blocks)
    shared = swapped(shared)
    pieces = exchanged(pieces)
    own, plus_far, minus_far, lower, higher = call(
        functools.partial(pack_body, DIRECT + NEAR[2:]),
        [bf16(DIAGS, 2, BS, BS)] + packed(DIRECT + NEAR[2:]),
        1,
        LAYERS,
    )(me, *pieces)
    plus_far = from_pair(plus_far, FAR_PAIRS)
    minus_far = from_pair(minus_far, -FAR_PAIRS)
    lower, higher = from_pair(lower, -2), from_pair(higher, 2)
    some = [shared, own]
    some = call(resplit_body, [shared_quarter] * LAYERS, 1, len(some))(me, *some)
    some = exchanged(some)
    band = call(fan_body, packed([FAN])[0], 1, LAYERS)(me, *some)
    plus_band, minus_band = far_across(band, FAR_PAIRS), far_across(band, -FAR_PAIRS)
    before = [own, band]
    before += [lower, higher]
    low, high = call(near_body, packed(NEAR[:2]), 0, len(before))(*before)
    low, high = from_pair(low, -1), from_pair(high, 1)
    arrived = [plus_far, minus_far, plus_band, minus_band]
    edge_low, edge_high = call(
        edge_body, packed([EDGE_LOW, EDGE_HIGH]), 0, len(arrived)
    )(*arrived)
    edge_low, edge_high = from_pair(edge_low, -1), from_pair(edge_high, 1)
    near = [own, low, high, lower, higher]
    right, partial = call(
        near_product_body,
        [bf16(NEAR_END, WIDTH), jax.ShapeDtypeStruct((2 * BS, WIDTH), jnp.float32)],
        0,
        len(near),
        scratch=[pltpu.VMEM((2 * BS, NEAR_END), jnp.bfloat16)],
    )(*near)
    results = call(
        purify_body,
        [quarter] * LAYERS,
        2,
        3 + len(ARRIVE) - NEAR_SOURCES,
        scratch=[
            pltpu.VMEM((WIDTH - NEAR_END, WIDTH), jnp.bfloat16),
            pltpu.VMEM((2 * BS, WIDTH), jnp.bfloat16),
            pltpu.VMEM((DIAGS, 2, BS, BS), jnp.bfloat16),
        ],
        flops=4 * 160 * 2 * BS**3,
    )(me, presence, own, right, partial, *arrived, edge_low, edge_high)
    results = exchanged(results)
    return call(join_body, bf16(DIAGS, 2 * LAYERS, BS // LAYERS, BS), 1, LAYERS)(
        me, *results
    )


def solution(mesh):
    placed = (P(None, ("row", "col"), "layer", None), P(None, ("row", "col")))
    return jax.shard_map(
        per_device,
        mesh=mesh,
        in_specs=placed,
        out_specs=P(None, ("row", "col"), "layer", None),
        check_vma=False,
    )
```

```python
import functools

import jax
import jax.numpy as jnp
from jax import lax
from jax.experimental import pallas as pl
from jax.experimental.pallas import tpu as pltpu
from jax.sharding import PartitionSpec as P

NBG = 512
BAND = 3
FAR = 160
BS = 128
LAYERS = 4
PAIRS = NBG // 2
FAR_PAIRS = FAR // 2
AXES = ("layer", "row", "col")
OFFSETS = list(range(-BAND, BAND + 1)) + [
    FAR - 1, FAR, FAR + 1, -FAR - 1, -FAR, -FAR + 1,
]
DIAGS = len(OFFSETS)
OFFSET_SET = {value % NBG for value in OFFSETS}

REACH = (
    list(range(-BAND, BAND + 2))
    + list(range(FAR - 1, FAR + 3))
    + list(range(-FAR - 1, -FAR + 3))
)
SLOT = {value % NBG: index for index, value in enumerate(REACH)}
NEAR_END = 8 * BS
PLUS_END = 12 * BS
WIDTH = 16 * BS


def needed(j):
    found = set()
    for i in range(2):
        for left in OFFSETS:
            if (i + left - j) % NBG == 0:
                for b, right in enumerate(OFFSETS):
                    if (left + right) % NBG in OFFSET_SET:
                        found.add(b)
    return sorted(found)


BANDS = range(2 * BAND + 1)
SHARED = sorted(b for b in set().union(*(needed(FAR + t) for t in range(-1, 3))) if b in BANDS)


def band_of(j):
    return [b for b in needed(j) if b in BANDS]


def far_of(j):
    return [b for b in needed(j) if b not in BANDS]


def tiles(rows, which=needed):
    return [(j, b) for j in rows for b in which(j)]


OWN = [(t, b) for b in range(DIAGS) for t in range(2)]
LOW, HIGH = tiles([-2, -1]), tiles([2, 3])
LOWER, HIGHER = tiles([-3]), tiles([4])
FAN = [(FAR + t, b) for t in range(2) for b in SHARED]
PLUS_BAND = FAN
MINUS_BAND = [(j - 2 * FAR, b) for j, b in FAN]
PLUS_FAR = tiles([FAR, FAR + 1], far_of)
MINUS_FAR = tiles([-FAR, -FAR + 1], far_of)
EDGE_LOW = tiles([FAR - 1, -FAR - 1])
EDGE_HIGH = tiles([FAR + 2, -FAR + 2])
MAIN = [PLUS_FAR, MINUS_FAR, PLUS_BAND, MINUS_BAND]
ARRIVE = [OWN, LOW, HIGH, LOWER, HIGHER] + MAIN + [EDGE_LOW, EDGE_HIGH]
NEAR = [[(j % 2, b) for j, b in message] for message in (LOW, HIGH, LOWER, HIGHER)]
DIRECT = [[(j % 2, b) for j, b in message] for message in (PLUS_FAR, MINUS_FAR)]


def place_of(p):
    return p % LAYERS * (PAIRS // LAYERS) + p // LAYERS


def moved(x, source_of):
    route = [(place_of(source_of(p)), place_of(p)) for p in range(PAIRS)]
    return lax.ppermute(x, AXES, route)


def across(p):
    cols = LAYERS * 8
    return p - p % cols + (p + cols // 2) % cols


def from_pair(x, distance):
    return moved(x, lambda p: (p + distance) % PAIRS)


def same_group(p, distance):
    return p - p % LAYERS + (p + distance) % LAYERS


def from_layer(x, distance):
    return moved(x, lambda p: same_group(p, distance))


def swapped(x):
    return moved(x, across)


def far_across(x, distance):
    return moved(x, lambda p: across((p + distance) % PAIRS))


def bf16(*shape):
    return jax.ShapeDtypeStruct(shape, jnp.bfloat16)


def call(body, out_shape, n_smem, n_vmem, scratch=(), flops=0, traffic=1 << 22):
    in_specs = [pl.BlockSpec(memory_space=pltpu.SMEM)] * n_smem
    in_specs += [pl.BlockSpec(memory_space=pltpu.VMEM)] * n_vmem
    return pl.pallas_call(
        body,
        out_shape=out_shape,
        in_specs=in_specs,
        out_specs=jax.tree.map(
            lambda _: pl.BlockSpec(memory_space=pltpu.VMEM), out_shape
        ),
        scratch_shapes=list(scratch),
        compiler_params=pltpu.CompilerParams(vmem_limit_bytes=24 << 20),
        cost_estimate=pl.CostEstimate(
            flops=flops, bytes_accessed=traffic, transcendentals=0
        ),
    )


def split_body(me_ref, presence_ref, blocks_ref, *out_refs):
    me = me_ref[0]
    shared_ref = out_refs[LAYERS]
    for s in range(LAYERS):
        other = lax.rem(me - s + LAYERS, LAYERS)
        for t in range(2):
            row = 2 * other + t
            for d in range(DIAGS):
                tile = blocks_ref[d, row]
                present = presence_ref[d, row] != 0
                tile = jnp.where(present, tile, jnp.zeros_like(tile))
                out_refs[s][d, t] = tile
                if d in SHARED:
                    shared_ref[SHARED.index(d), row] = tile


def resplit_body(me_ref, shared_ref, *out_refs):
    for s, out_ref in enumerate(out_refs[-LAYERS:]):
        row = 2 * lax.rem(me_ref[0] - s + LAYERS, LAYERS)
        for t in range(2):
            for k in range(len(SHARED)):
                out_ref[k, t] = shared_ref[k, row + t]


def gather_pieces(me, pieces, out_ref):
    for s, piece in enumerate(pieces):
        other = lax.rem(me + s, LAYERS)
        start = pl.multiple_of(other * (BS // LAYERS), BS // LAYERS)
        out_ref[:, :, pl.ds(start, BS // LAYERS), :] = piece[...]


def pack_body(messages, me_ref, *refs):
    pieces, own_ref, out_refs = refs[:LAYERS], refs[LAYERS], refs[LAYERS + 1 :]
    gather_pieces(me_ref[0], pieces, own_ref)
    for message, out_ref in zip(messages, out_refs):
        for k, (t, b) in enumerate(message):
            out_ref[k] = own_ref[b, t]


def near_body(own_ref, *refs):
    for message, out_ref in zip(NEAR[:2], refs[-2:]):
        for k, (t, b) in enumerate(message):
            out_ref[k] = own_ref[b, t]


def fan_body(me_ref, *refs):
    pieces, out_ref = refs[:LAYERS], refs[-1]
    for s, piece in enumerate(pieces):
        other = lax.rem(me_ref[0] + s, LAYERS)
        rows = pl.ds(pl.multiple_of(other * (BS // LAYERS), BS // LAYERS), BS // LAYERS)
        for k, (j, b) in enumerate(FAN):
            out_ref[k, rows, :] = piece[SHARED.index(b), j - FAR]


def edge_body(*refs):
    sources, out_refs = refs[: len(MAIN)], refs[len(MAIN) :]
    for shift, message, out_ref in zip((2, -2), (EDGE_LOW, EDGE_HIGH), out_refs):
        for k, (j, b) in enumerate(message):
            [(ref, held)] = [
                (ref, held)
                for ref, held in zip(sources, MAIN)
                if (j + shift, b) in held
            ]
            out_ref[k] = ref[held.index((j + shift, b))]


def placements():
    found = {}
    for operand, message in enumerate(ARRIVE):
        for k, (j, b) in enumerate(message):
            column = SLOT.get((j + OFFSETS[b]) % NBG)
            if column is not None:
                found[SLOT[j % NBG], column] = (operand, k if operand else (b, j))
    return found


NEAR_SOURCES = 5


def targets():
    return {
        (i, SLOT[(i + offset) % NBG]): d
        for i in range(2)
        for d, offset in enumerate(OFFSETS)
    }


def fill_right(out_ref, sources, first, rows):
    placed = placements()
    for row in rows:
        for column in range(16):
            where = (pl.ds((row - rows[0]) * BS, BS), pl.ds(column * BS, BS))
            if (row, column) in placed:
                operand, index = placed[row, column]
                out_ref[where] = sources[operand - first][index]
            else:
                out_ref[where] = jnp.zeros((BS, BS), jnp.bfloat16)


def fill_left(out_ref, own_ref, columns):
    for i in range(2):
        for column in columns:
            where = (pl.ds(i * BS, BS), pl.ds((column - columns[0]) * BS, BS))
            d = targets().get((i, column))
            if d is None:
                out_ref[where] = jnp.zeros((BS, BS), jnp.bfloat16)
            else:
                out_ref[where] = own_ref[d, i]


def dot(left, right):
    return jnp.dot(left, right, preferred_element_type=jnp.float32)


def near_product_body(*refs):
    sources, (right_ref, partial_ref, left_ref) = refs[:NEAR_SOURCES], refs[NEAR_SOURCES:]
    fill_right(right_ref, sources, 0, range(8))
    fill_left(left_ref, sources[0], range(8))
    for column in range(0, 16, 2):
        wide = pl.ds(column * BS, 2 * BS)
        partial_ref[:, wide] = dot(left_ref[...], right_ref[:, wide])


def purify_body(me_ref, presence_ref, own_ref, right_near_ref, partial_ref, *refs):
    fars = len(ARRIVE) - NEAR_SOURCES
    sources, outs = refs[:fars], refs[fars : fars + LAYERS]
    right_ref, left_ref, result_ref = refs[fars + LAYERS :]
    me = me_ref[0]
    fill_right(right_ref, sources, NEAR_SOURCES, range(8, 16))
    fill_left(left_ref, own_ref, range(16))

    def far_product(columns):
        start = columns[0] * BS
        wide = pl.ds(start, len(columns) * BS)
        if start < NEAR_END:
            return dot(left_ref[:, NEAR_END:], right_ref[:, wide])
        if start < PLUS_END:
            return dot(left_ref[:, NEAR_END:PLUS_END], right_ref[: PLUS_END - NEAR_END, wide])
        return dot(left_ref[:, PLUS_END:], right_ref[PLUS_END - NEAR_END :, wide])

    def near_product(columns):
        wide = pl.ds(columns[0] * BS, len(columns) * BS)
        return dot(left_ref[:, :NEAR_END], right_near_ref[:, wide])

    def each(columns, total, use):
        for at, column in enumerate(columns):
            for i in range(2):
                d = targets().get((i, column))
                if d is not None:
                    tile = total[i * BS : (i + 1) * BS, at * BS : (at + 1) * BS]
                    use(i, column, d, presence_ref[d, 2 * me + i] != 0, tile)

    groups = [[c, c + 1] for c in range(0, 16, 2)]

    def keep_second(i, column, d, present, tile):
        second = jnp.where(present, tile, jnp.zeros_like(tile)).astype(jnp.bfloat16)
        result_ref[d, i] = second

    for columns in groups:
        partial = partial_ref[:, pl.ds(columns[0] * BS, len(columns) * BS)]
        each(columns, partial + far_product(columns), keep_second)
    for (i, column), d in targets().items():
        left_ref[pl.ds(i * BS, BS), pl.ds(column * BS, BS)] = result_ref[d, i]

    def keep_result(i, column, d, present, tile):
        third = jnp.where(present, tile, jnp.zeros_like(tile))
        second = result_ref[d, i].astype(jnp.float32)
        result_ref[d, i] = (3.0 * second - 2.0 * third).astype(jnp.bfloat16)

    for columns in groups:
        each(columns, near_product(columns) + far_product(columns), keep_result)
    for s, out_ref in enumerate(outs):
        other = lax.rem(me - s + LAYERS, LAYERS)
        start = pl.multiple_of(other * (BS // LAYERS), BS // LAYERS)
        out_ref[...] = result_ref[:, :, pl.ds(start, BS // LAYERS), :]


def join_body(me_ref, *refs):
    me = me_ref[0]
    out_ref = refs[LAYERS]
    for s in range(LAYERS):
        row = 2 * lax.rem(me + s, LAYERS)
        for t in range(2):
            for d in range(DIAGS):
                out_ref[d, row + t] = refs[s][d, t]


def exchanged(pieces):
    far = from_layer(pieces[2], 2)
    return [pieces[0], from_layer(pieces[1], 1), far, from_layer(pieces[3], 3)]


def per_device(blocks, presence):
    me = lax.axis_index("layer").astype(jnp.int32).reshape(1)

    def packed(messages):
        return [bf16(len(message), BS, BS) for message in messages]

    quarter = bf16(DIAGS, 2, BS // LAYERS, BS)
    shared_quarter = bf16(len(SHARED), 2, BS // LAYERS, BS)
    *pieces, shared = call(
        split_body,
        [quarter] * LAYERS + [bf16(len(SHARED), 2 * LAYERS, BS // LAYERS, BS)],
        2,
        1,
    )(me, presence, blocks)
    shared = swapped(shared)
    pieces = exchanged(pieces)
    own, plus_far, minus_far, lower, higher = call(
        functools.partial(pack_body, DIRECT + NEAR[2:]),
        [bf16(DIAGS, 2, BS, BS)] + packed(DIRECT + NEAR[2:]),
        1,
        LAYERS,
    )(me, *pieces)
    plus_far = from_pair(plus_far, FAR_PAIRS)
    minus_far = from_pair(minus_far, -FAR_PAIRS)
    lower, higher = from_pair(lower, -2), from_pair(higher, 2)
    some = [shared, own]
    some = call(resplit_body, [shared_quarter] * LAYERS, 1, len(some))(me, *some)
    some = exchanged(some)
    band = call(fan_body, packed([FAN])[0], 1, LAYERS + 1)(me, *some, higher)
    plus_band, minus_band = far_across(band, FAR_PAIRS), far_across(band, -FAR_PAIRS)
    before = [own, band]
    before += [lower]
    low, high = call(near_body, packed(NEAR[:2]), 0, len(before))(*before)
    low, high = from_pair(low, -1), from_pair(high, 1)
    arrived = [plus_far, minus_far, plus_band, minus_band]
    edge_low, edge_high = call(
        edge_body, packed([EDGE_LOW, EDGE_HIGH]), 0, len(arrived)
    )(*arrived)
    edge_low, edge_high = from_pair(edge_low, -1), from_pair(edge_high, 1)
    near = [own, low, high, lower, higher]
    right, partial = call(
        near_product_body,
        [bf16(NEAR_END, WIDTH), jax.ShapeDtypeStruct((2 * BS, WIDTH), jnp.float32)],
        0,
        len(near),
        scratch=[pltpu.VMEM((2 * BS, NEAR_END), jnp.bfloat16)],
    )(*near)
    results = call(
        purify_body,
        [quarter] * LAYERS,
        2,
        3 + len(ARRIVE) - NEAR_SOURCES,
        scratch=[
            pltpu.VMEM((WIDTH - NEAR_END, WIDTH), jnp.bfloat16),
            pltpu.VMEM((2 * BS, WIDTH), jnp.bfloat16),
            pltpu.VMEM((DIAGS, 2, BS, BS), jnp.bfloat16),
        ],
        flops=4 * 160 * 2 * BS**3,
    )(me, presence, own, right, partial, *arrived, edge_low, edge_high)
    results = exchanged(results)
    return call(join_body, bf16(DIAGS, 2 * LAYERS, BS // LAYERS, BS), 1, LAYERS)(
        me, *results
    )


def solution(mesh):
    placed = (P(None, ("row", "col"), "layer", None), P(None, ("row", "col")))
    return jax.shard_map(
        per_device,
        mesh=mesh,
        in_specs=placed,
        out_specs=P(None, ("row", "col"), "layer", None),
        check_vma=False,
    )
```

```python
import functools

import jax
import jax.numpy as jnp
from jax import lax
from jax.experimental import pallas as pl
from jax.experimental.pallas import tpu as pltpu
from jax.sharding import PartitionSpec as P

NBG = 512
BAND = 3
FAR = 160
BS = 128
LAYERS = 4
PAIRS = NBG // 2
FAR_PAIRS = FAR // 2
AXES = ("layer", "row", "col")
OFFSETS = list(range(-BAND, BAND + 1)) + [
    FAR - 1, FAR, FAR + 1, -FAR - 1, -FAR, -FAR + 1,
]
DIAGS = len(OFFSETS)
OFFSET_SET = {value % NBG for value in OFFSETS}

REACH = (
    list(range(-BAND, BAND + 2))
    + list(range(FAR - 1, FAR + 3))
    + list(range(-FAR - 1, -FAR + 3))
)
SLOT = {value % NBG: index for index, value in enumerate(REACH)}
NEAR_END = 8 * BS
PLUS_END = 12 * BS
WIDTH = 16 * BS


def needed(j):
    found = set()
    for i in range(2):
        for left in OFFSETS:
            if (i + left - j) % NBG == 0:
                for b, right in enumerate(OFFSETS):
                    if (left + right) % NBG in OFFSET_SET:
                        found.add(b)
    return sorted(found)


BANDS = range(2 * BAND + 1)
SHARED = sorted(b for b in set().union(*(needed(FAR + t) for t in range(-1, 3))) if b in BANDS)


def band_of(j):
    return [b for b in needed(j) if b in BANDS]


def far_of(j):
    return [b for b in needed(j) if b not in BANDS]


def tiles(rows, which=needed):
    return [(j, b) for j in rows for b in which(j)]


OWN = [(t, b) for b in range(DIAGS) for t in range(2)]
LOW, HIGH = tiles([-2, -1]), tiles([2, 3])
LOWER, HIGHER = tiles([-3]), tiles([4])
FAN = [(FAR + t, b) for t in range(2) for b in SHARED]
PLUS_BAND = FAN
MINUS_BAND = [(j - 2 * FAR, b) for j, b in FAN]
PLUS_FAR = tiles([FAR, FAR + 1], far_of)
MINUS_FAR = tiles([-FAR, -FAR + 1], far_of)
EDGE_LOW = tiles([FAR - 1, -FAR - 1])
EDGE_HIGH = tiles([FAR + 2, -FAR + 2])
MAIN = [PLUS_FAR, MINUS_FAR, PLUS_BAND, MINUS_BAND]
ARRIVE = [OWN, LOW, HIGH, LOWER, HIGHER] + MAIN + [EDGE_LOW, EDGE_HIGH]
NEAR = [[(j % 2, b) for j, b in message] for message in (LOW, HIGH, LOWER, HIGHER)]
DIRECT = [[(j % 2, b) for j, b in message] for message in (PLUS_FAR, MINUS_FAR)]


def place_of(p):
    return p % LAYERS * (PAIRS // LAYERS) + p // LAYERS


def moved(x, source_of):
    route = [(place_of(source_of(p)), place_of(p)) for p in range(PAIRS)]
    return lax.ppermute(x, AXES, route)


def across(p):
    cols = LAYERS * 8
    return p - p % cols + (p + cols // 2) % cols


def from_pair(x, distance):
    return moved(x, lambda p: (p + distance) % PAIRS)


def same_group(p, distance):
    return p - p % LAYERS + (p + distance) % LAYERS


def from_layer(x, distance):
    return moved(x, lambda p: same_group(p, distance))


def swapped(x):
    return moved(x, across)


def far_across(x, distance):
    return moved(x, lambda p: across((p + distance) % PAIRS))


def bf16(*shape):
    return jax.ShapeDtypeStruct(shape, jnp.bfloat16)


def call(body, out_shape, n_smem, n_vmem, scratch=(), flops=0, traffic=1 << 22):
    in_specs = [pl.BlockSpec(memory_space=pltpu.SMEM)] * n_smem
    in_specs += [pl.BlockSpec(memory_space=pltpu.VMEM)] * n_vmem
    return pl.pallas_call(
        body,
        out_shape=out_shape,
        in_specs=in_specs,
        out_specs=jax.tree.map(
            lambda _: pl.BlockSpec(memory_space=pltpu.VMEM), out_shape
        ),
        scratch_shapes=list(scratch),
        compiler_params=pltpu.CompilerParams(vmem_limit_bytes=24 << 20),
        cost_estimate=pl.CostEstimate(
            flops=flops, bytes_accessed=traffic, transcendentals=0
        ),
    )


def split_body(me_ref, presence_ref, blocks_ref, *out_refs):
    me = me_ref[0]
    shared_ref = out_refs[LAYERS]
    for s in range(LAYERS):
        other = lax.rem(me - s + LAYERS, LAYERS)
        for t in range(2):
            row = 2 * other + t
            for d in range(DIAGS):
                tile = blocks_ref[d, row]
                present = presence_ref[d, row] != 0
                tile = jnp.where(present, tile, jnp.zeros_like(tile))
                out_refs[s][d, t] = tile
                if d in SHARED:
                    shared_ref[SHARED.index(d), row] = tile


def resplit_body(me_ref, shared_ref, *out_refs):
    for s, out_ref in enumerate(out_refs[-LAYERS:]):
        row = 2 * lax.rem(me_ref[0] - s + LAYERS, LAYERS)
        for t in range(2):
            for k in range(len(SHARED)):
                out_ref[k, t] = shared_ref[k, row + t]


def gather_pieces(me, pieces, out_ref):
    for s, piece in enumerate(pieces):
        other = lax.rem(me + s, LAYERS)
        start = pl.multiple_of(other * (BS // LAYERS), BS // LAYERS)
        out_ref[:, :, pl.ds(start, BS // LAYERS), :] = piece[...]


def pack_body(messages, me_ref, *refs):
    pieces, own_ref, out_refs = refs[:LAYERS], refs[LAYERS], refs[LAYERS + 1 :]
    gather_pieces(me_ref[0], pieces, own_ref)
    for message, out_ref in zip(messages, out_refs):
        for k, (t, b) in enumerate(message):
            out_ref[k] = own_ref[b, t]


def near_body(own_ref, *refs):
    for message, out_ref in zip(NEAR[:2], refs[-2:]):
        for k, (t, b) in enumerate(message):
            out_ref[k] = own_ref[b, t]


def fan_body(me_ref, *refs):
    pieces, out_ref = refs[:LAYERS], refs[-1]
    for s, piece in enumerate(pieces):
        other = lax.rem(me_ref[0] + s, LAYERS)
        rows = pl.ds(pl.multiple_of(other * (BS // LAYERS), BS // LAYERS), BS // LAYERS)
        for k, (j, b) in enumerate(FAN):
            out_ref[k, rows, :] = piece[SHARED.index(b), j - FAR]


def edge_body(*refs):
    sources, out_refs = refs[: len(MAIN)], refs[len(MAIN) :]
    for shift, message, out_ref in zip((2, -2), (EDGE_LOW, EDGE_HIGH), out_refs):
        for k, (j, b) in enumerate(message):
            [(ref, held)] = [
                (ref, held)
                for ref, held in zip(sources, MAIN)
                if (j + shift, b) in held
            ]
            out_ref[k] = ref[held.index((j + shift, b))]


def placements():
    found = {}
    for operand, message in enumerate(ARRIVE):
        for k, (j, b) in enumerate(message):
            column = SLOT.get((j + OFFSETS[b]) % NBG)
            if column is not None:
                found[SLOT[j % NBG], column] = (operand, k if operand else (b, j))
    return found


NEAR_SOURCES = 5


def targets():
    return {
        (i, SLOT[(i + offset) % NBG]): d
        for i in range(2)
        for d, offset in enumerate(OFFSETS)
    }


def fill_right(out_ref, sources, first, rows):
    placed = placements()
    for row in rows:
        for column in range(16):
            where = (pl.ds((row - rows[0]) * BS, BS), pl.ds(column * BS, BS))
            if (row, column) in placed:
                operand, index = placed[row, column]
                out_ref[where] = sources[operand - first][index]
            else:
                out_ref[where] = jnp.zeros((BS, BS), jnp.bfloat16)


def fill_left(out_ref, own_ref, columns):
    for i in range(2):
        for column in columns:
            where = (pl.ds(i * BS, BS), pl.ds((column - columns[0]) * BS, BS))
            d = targets().get((i, column))
            if d is None:
                out_ref[where] = jnp.zeros((BS, BS), jnp.bfloat16)
            else:
                out_ref[where] = own_ref[d, i]


def dot(left, right):
    return jnp.dot(left, right, preferred_element_type=jnp.float32)


def near_product_body(*refs):
    sources, (right_ref, partial_ref, left_ref) = refs[:NEAR_SOURCES], refs[NEAR_SOURCES:]
    fill_right(right_ref, sources, 0, range(8))
    fill_left(left_ref, sources[0], range(8))
    for column in range(0, 16, 2):
        wide = pl.ds(column * BS, 2 * BS)
        partial_ref[:, wide] = dot(left_ref[...], right_ref[:, wide])


def purify_body(me_ref, presence_ref, own_ref, right_near_ref, partial_ref, *refs):
    fars = len(ARRIVE) - NEAR_SOURCES
    sources, outs = refs[:fars], refs[fars : fars + LAYERS]
    right_ref, left_ref, result_ref = refs[fars + LAYERS :]
    me = me_ref[0]
    fill_right(right_ref, sources, NEAR_SOURCES, range(8, 16))
    fill_left(left_ref, own_ref, range(16))

    def far_product(columns):
        start = columns[0] * BS
        wide = pl.ds(start, len(columns) * BS)
        if start < NEAR_END:
            return dot(left_ref[:, NEAR_END:], right_ref[:, wide])
        if start < PLUS_END:
            return dot(left_ref[:, NEAR_END:PLUS_END], right_ref[: PLUS_END - NEAR_END, wide])
        return dot(left_ref[:, PLUS_END:], right_ref[PLUS_END - NEAR_END :, wide])

    def near_product(columns):
        wide = pl.ds(columns[0] * BS, len(columns) * BS)
        first = 2 * BS if columns[0] in (6, 10, 14) else 0
        last = NEAR_END - 2 * BS if columns[0] in (0, 8, 12) else NEAR_END
        return dot(left_ref[:, first:last], right_near_ref[first:last, wide])

    def each(columns, total, use):
        for at, column in enumerate(columns):
            for i in range(2):
                d = targets().get((i, column))
                if d is not None:
                    tile = total[i * BS : (i + 1) * BS, at * BS : (at + 1) * BS]
                    use(i, column, d, presence_ref[d, 2 * me + i] != 0, tile)

    groups = [[c, c + 1] for c in range(0, 16, 2)]

    def keep_second(i, column, d, present, tile):
        second = jnp.where(present, tile, jnp.zeros_like(tile)).astype(jnp.bfloat16)
        result_ref[d, i] = second

    for columns in groups:
        partial = partial_ref[:, pl.ds(columns[0] * BS, len(columns) * BS)]
        each(columns, partial + far_product(columns), keep_second)
    for (i, column), d in targets().items():
        left_ref[pl.ds(i * BS, BS), pl.ds(column * BS, BS)] = result_ref[d, i]

    def keep_result(i, column, d, present, tile):
        third = jnp.where(present, tile, jnp.zeros_like(tile))
        second = result_ref[d, i].astype(jnp.float32)
        result_ref[d, i] = (3.0 * second - 2.0 * third).astype(jnp.bfloat16)

    for columns in groups:
        each(columns, near_product(columns) + far_product(columns), keep_result)
    for s, out_ref in enumerate(outs):
        other = lax.rem(me - s + LAYERS, LAYERS)
        start = pl.multiple_of(other * (BS // LAYERS), BS // LAYERS)
        out_ref[...] = result_ref[:, :, pl.ds(start, BS // LAYERS), :]


def join_body(me_ref, *refs):
    me = me_ref[0]
    out_ref = refs[LAYERS]
    for s in range(LAYERS):
        row = 2 * lax.rem(me + s, LAYERS)
        for t in range(2):
            for d in range(DIAGS):
                out_ref[d, row + t] = refs[s][d, t]


def exchanged(pieces):
    far = from_layer(pieces[2], 2)
    return [pieces[0], from_layer(pieces[1], 1), far, from_layer(pieces[3], 3)]


def per_device(blocks, presence):
    me = lax.axis_index("layer").astype(jnp.int32).reshape(1)

    def packed(messages):
        return [bf16(len(message), BS, BS) for message in messages]

    quarter = bf16(DIAGS, 2, BS // LAYERS, BS)
    shared_quarter = bf16(len(SHARED), 2, BS // LAYERS, BS)
    *pieces, shared = call(
        split_body,
        [quarter] * LAYERS + [bf16(len(SHARED), 2 * LAYERS, BS // LAYERS, BS)],
        2,
        1,
    )(me, presence, blocks)
    shared = swapped(shared)
    pieces = exchanged(pieces)
    own, plus_far, minus_far, lower, higher = call(
        functools.partial(pack_body, DIRECT + NEAR[2:]),
        [bf16(DIAGS, 2, BS, BS)] + packed(DIRECT + NEAR[2:]),
        1,
        LAYERS,
    )(me, *pieces)
    plus_far = from_pair(plus_far, FAR_PAIRS)
    minus_far = from_pair(minus_far, -FAR_PAIRS)
    lower, higher = from_pair(lower, -2), from_pair(higher, 2)
    some = [shared, own]
    some = call(resplit_body, [shared_quarter] * LAYERS, 1, len(some))(me, *some)
    some = exchanged(some)
    band = call(fan_body, packed([FAN])[0], 1, LAYERS + 1)(me, *some, higher)
    plus_band, minus_band = far_across(band, FAR_PAIRS), far_across(band, -FAR_PAIRS)
    before = [own, band]
    before += [lower]
    low, high = call(near_body, packed(NEAR[:2]), 0, len(before))(*before)
    low, high = from_pair(low, -1), from_pair(high, 1)
    arrived = [plus_far, minus_far, plus_band, minus_band]
    edge_low, edge_high = call(
        edge_body, packed([EDGE_LOW, EDGE_HIGH]), 0, len(arrived)
    )(*arrived)
    edge_low, edge_high = from_pair(edge_low, -1), from_pair(edge_high, 1)
    near = [own, low, high, lower, higher]
    right, partial = call(
        near_product_body,
        [bf16(NEAR_END, WIDTH), jax.ShapeDtypeStruct((2 * BS, WIDTH), jnp.float32)],
        0,
        len(near),
        scratch=[pltpu.VMEM((2 * BS, NEAR_END), jnp.bfloat16)],
    )(*near)
    results = call(
        purify_body,
        [quarter] * LAYERS,
        2,
        3 + len(ARRIVE) - NEAR_SOURCES,
        scratch=[
            pltpu.VMEM((WIDTH - NEAR_END, WIDTH), jnp.bfloat16),
            pltpu.VMEM((2 * BS, WIDTH), jnp.bfloat16),
            pltpu.VMEM((DIAGS, 2, BS, BS), jnp.bfloat16),
        ],
        flops=4 * 160 * 2 * BS**3,
    )(me, presence, own, right, partial, *arrived, edge_low, edge_high)
    results = exchanged(results)
    return call(join_body, bf16(DIAGS, 2 * LAYERS, BS // LAYERS, BS), 1, LAYERS)(
        me, *results
    )


def solution(mesh):
    placed = (P(None, ("row", "col"), "layer", None), P(None, ("row", "col")))
    return jax.shard_map(
        per_device,
        mesh=mesh,
        in_specs=placed,
        out_specs=P(None, ("row", "col"), "layer", None),
        check_vma=False,
    )
```
